256 devices in a mesh: stream: 32 (over x, z), span: 8 (over y, core).
Axes of the slice: x: 4, y: 4, z: 8, core: 2. Of those that a mesh axis runs over, the one named last changes fastest.
Arguments:
- state: float32 [5, 8, 512, 1024], P(None, None, 'stream', 'span'), may hold values from -0.3 to 3, as said below
Outputs:
- state_next: float32 [5, 8, 512, 1024], P(None, None, 'stream', 'span')
- flux_difference: float32 [5, 8, 512, 1024], P(None, None, 'stream', 'span')
The draws below stay inside these ranges and needn't reach their ends.
Inputs may be any that keep to these rules, and one draw needn't show every extreme that they name: Each cell holds a gas state with density from 0.55 to 1.65, streamwise velocity from 0.2 to 0.6, spanwise and wall-normal velocities within 0.15 of zero and pressure from 0.55 to 1.0.
All inputs are finite; a program needn't handle non-finite values.
Results may differ from the reference program's by a relative error of at most 0.002.
Values sent between devices are 32-bit elements; how exact they have to be, the bound alone decides.
A program may use at most 128 MiB of HBM per device.

```python
import jax
import jax.numpy as jnp
from jax import lax

CX = 16
NZ = 8
NX = 512
NY = 1024


def draw_state(key, part):
    folded = jax.random.fold_in(key, 7)
    subkeys = jax.random.split(folded, 6)
    grid_shape = (NZ, NX, NY)
    uniforms = [jax.random.uniform(subkeys[field_id], grid_shape, jnp.float32) for field_id in range(5)]
    density = 0.6 + 0.8 * uniforms[0]
    speed_x = 0.25 + 0.3 * uniforms[1]
    pressure = 0.6 + 0.4 * uniforms[4]
    speed_y = 0.3 * (uniforms[2] - 0.5)
    speed_z = 0.3 * (uniforms[3] - 0.5)
    energy = pressure / 0.4 + 0.5 * density * (speed_x * speed_x + speed_y * speed_y + speed_z * speed_z)
    return jnp.stack([density, density * speed_x, density * speed_y, density * speed_z, energy])


def setup_inputs(seed: int = 0) -> dict:
    streams_of = jax.random.split(jax.random.key(seed), 2)
    state = draw_state(jax.random.fold_in(streams_of[1], 71), 0)
    return dict(state=state)


GAMMA = 1.4
GAMMA_LESS = 0.4
DAMPING = 0.125
DIAGONAL = 1.25

def primitives(fields):
    density = fields[0]
    speed_x = fields[1] / density
    speed_y = fields[2] / density
    speed_z = fields[3] / density
    kinetic = 0.5 * (speed_x * speed_x + speed_y * speed_y + speed_z * speed_z)
    pressure = GAMMA_LESS * (fields[4] - density * kinetic)
    return (density, speed_x, speed_y, speed_z, kinetic, pressure)

def flux_along(fields, direction):
    density, speed_x, speed_y, speed_z, kinetic, pressure = primitives(fields)
    normal_speed = (speed_x, speed_y, speed_z)[direction - 1]
    mass_flow = density * normal_speed
    columns = [mass_flow, mass_flow * speed_x, mass_flow * speed_y, mass_flow * speed_z, normal_speed * (fields[4] + pressure)]
    columns[direction] = columns[direction] + pressure
    return jnp.stack(columns)

def jacobian_rows(fields):
    density, speed_x, speed_y, speed_z, kinetic, pressure = primitives(fields)
    enthalpy = (fields[4] + pressure) / density
    zero_entry = jnp.zeros_like(density)
    unit_entry = jnp.ones_like(density)
    gas_kinetic = GAMMA_LESS * kinetic
    return [[zero_entry, unit_entry, zero_entry, zero_entry, zero_entry], [gas_kinetic - speed_x * speed_x, (3.0 - GAMMA) * speed_x, -GAMMA_LESS * speed_y, -GAMMA_LESS * speed_z, GAMMA_LESS * unit_entry], [-speed_x * speed_y, speed_y, speed_x, zero_entry, zero_entry], [-speed_x * speed_z, speed_z, zero_entry, speed_x, zero_entry], [speed_x * (gas_kinetic - enthalpy), enthalpy - GAMMA_LESS * speed_x * speed_x, -GAMMA_LESS * speed_x * speed_y, -GAMMA_LESS * speed_x * speed_z, GAMMA * speed_x]]

def jacobian(fields):
    return jnp.stack([jnp.stack(matrix_row) for matrix_row in jacobian_rows(fields)])

def jacobian_apply(fields, vector):
    result = []
    for matrix_row in jacobian_rows(fields):
        running_sum = matrix_row[0] * vector[0]
        for column in range(1, 5):
            running_sum = running_sum + matrix_row[column] * vector[column]
        result.append(running_sum)
    return jnp.stack(result)

def matmul_small(left_block, right_block):
    return lax.optimization_barrier(jnp.sum(left_block[:, :, None] * right_block[None], axis=1))

def identity_like(matrix):
    return jnp.eye(5, dtype=matrix.dtype).reshape((5, 5) + (1,) * (matrix.ndim - 2))

def solve_small(matrix, targets):
    normal_matrix = {}
    for row_id in range(5):
        for col_id in range(row_id + 1):
            normal_matrix[row_id, col_id] = lax.optimization_barrier(jnp.sum(matrix[:, row_id] * matrix[:, col_id], axis=0))
    projected = [lax.optimization_barrier(jnp.sum(matrix[:, row_id][:, None] * targets, axis=0)) for row_id in range(5)]
    factor_entries = {}
    inverse = []
    for row_id in range(5):
        for col_id in range(row_id + 1):
            current = normal_matrix[row_id, col_id]
            for mid_id in range(col_id):
                current = current - factor_entries[row_id, mid_id] * factor_entries[col_id, mid_id]
            if row_id == col_id:
                inverse.append(1.0 / jnp.sqrt(current))
            else:
                factor_entries[row_id, col_id] = current * inverse[col_id]
    forward = []
    for row_id in range(5):
        current = projected[row_id]
        for mid_id in range(row_id):
            current = current - factor_entries[row_id, mid_id][None] * forward[mid_id]
        forward.append(current * inverse[row_id][None])
    solution = [None] * 5
    for row_id in reversed(range(5)):
        current = forward[row_id]
        for mid_id in range(row_id + 1, 5):
            current = current - factor_entries[mid_id, row_id][None] * solution[mid_id]
        solution[row_id] = current * inverse[row_id][None]
    return jnp.stack(solution)

def thomas_step(running, inputs):
    factor, partial_value = running
    near_block, far_block, source = inputs
    pivot_block = DIAGONAL * identity_like(near_block) - matmul_small(near_block, factor)
    columns = jnp.concatenate([far_block, source - matmul_small(near_block, partial_value)], axis=1)
    solved = solve_small(pivot_block, columns)
    updated = (solved[:, :5], solved[:, 5:])
    return (updated, updated)

def back_step(following, inputs):
    factor, partial_value = inputs
    current = partial_value - matmul_small(factor, following)
    return (current, current)

def couplings(ext_plane, courant):
    blocks = jacobian(ext_plane)
    identity_block = identity_like(blocks)
    lower_rows = -(0.5 * courant) * blocks[:, :, :-2] - DAMPING * identity_block
    upper_rows = 0.5 * courant * blocks[:, :, 2:] - DAMPING * identity_block
    return (jnp.moveaxis(lower_rows, 2, 0), jnp.moveaxis(upper_rows, 2, 0))

def right_side(state, stream_padded, flux_padded, span_padded, courant):
    flux_step = flux_padded[:, :, 2:] - flux_padded[:, :, :-2]
    curvature = stream_padded[:, :, 2:] - 2.0 * state + stream_padded[:, :, :-2]
    span_flux = flux_along(span_padded, 2)
    span_step = (-span_flux[..., 4:] + 8.0 * span_flux[..., 3:-1] - 8.0 * span_flux[..., 1:-3] + span_flux[..., :-4]) / 12.0
    mirror = jnp.array([1.0, 1.0, 1.0, -1.0, 1.0], dtype=state.dtype).reshape(5, 1, 1, 1)
    normal_padded = jnp.concatenate([state[:, :1] * mirror, state, state[:, -1:]], axis=1)
    normal_flux = flux_along(normal_padded, 3)
    normal_step = 0.5 * (normal_flux[:, 2:] - normal_flux[:, :-2])
    return -(0.5 * courant) * flux_step + DAMPING * curvature - span_step - normal_step

def reference(state):
    courant = 4.0 * CX
    widths = ((0, 0), (0, 0), (1, 1), (0, 0))
    stream_padded = jnp.pad(state, widths)
    flux_padded = jnp.pad(flux_along(state, 1), widths)
    span_padded = jnp.concatenate([state[..., -2:], state, state[..., :2]], axis=3)
    source = right_side(state, stream_padded, flux_padded, span_padded, courant)
    resting = jnp.array([1.0, 0.0, 0.0, 0.0, 2.5], dtype=state.dtype).reshape(5, 1, 1, 1)
    resting = jnp.broadcast_to(resting, (5, state.shape[1], 1, state.shape[3]))
    extended = jnp.concatenate([resting, state, resting], axis=2)

    def solve_plane(plane_inputs):
        ext_plane, source_plane = plane_inputs
        lower_rows, upper_rows = couplings(ext_plane, courant)
        source_rows = jnp.moveaxis(source_plane, 1, 0)[:, :, None]
        start = (jnp.zeros_like(lower_rows[0]), jnp.zeros_like(source_rows[0]))
        ignored, stored = lax.scan(thomas_step, start, (lower_rows, upper_rows, source_rows))
        ignored_last, values = lax.scan(back_step, jnp.zeros_like(source_rows[0]), stored, reverse=True)
        return jnp.moveaxis(values[:, :, 0], 0, 1)
    update = lax.map(solve_plane, (jnp.moveaxis(extended, 1, 0), jnp.moveaxis(source, 1, 0)))
    update = jnp.moveaxis(update, 0, 1)
    state_next = state + update
    linear_flux = jacobian_apply(state, state_next)
    linear_padded = jnp.pad(linear_flux, widths)
    flux_difference = -0.5 * (linear_padded[:, :, 2:] - linear_padded[:, :, :-2])
    return (state_next, flux_difference)
```

```python
import jax
import jax.numpy as jnp
from jax import lax
from jax.experimental import pallas as pl
from jax.experimental.pallas import tpu as pltpu
from jax.sharding import PartitionSpec as P

MESH = pl.DeviceIdType.MESH
N = 32
SPAN = 8
CX = 16
DISS = 1.0 / 256.0
DIAG = 1.25 / 819.2
PIVOTS = (1, 2, 3, 0, 4)
ROWS = 16
BACK_ROWS = 8
F32 = jnp.float32


def mul(a, b):
    if a is None or b is None:
        return None
    if isinstance(a, float) and a == 1.0:
        return b
    if isinstance(b, float) and b == 1.0:
        return a
    return a * b


def add(a, b):
    if a is None:
        return b
    if b is None:
        return a
    return a + b


def sub(a, b):
    if b is None:
        return a
    if a is None:
        return -b
    return a - b


def primitives(s):
    inv = 1.0 / s[0]
    u, v, w = s[1] * inv, s[2] * inv, s[3] * inv
    k = 0.5 * (u * u + v * v + w * w)
    p = 0.4 * (s[4] - s[0] * k)
    return u, v, w, k, p, (s[4] + p) * inv


def apply_jacobian(cell, sign, x):
    u, v, w, k, h = cell
    us = u + sign * DISS if sign else u
    q = sub(x[1], mul(u, x[0]))
    inner = sub(mul(k, x[0]), mul(u, x[1]))
    inner = sub(sub(inner, mul(v, x[2])), mul(w, x[3]))
    p = mul(0.4, add(inner, x[4]))
    top = x[1]
    if sign and x[0] is not None:
        top = add(top, mul(sign * DISS, x[0]))
    return [
        top,
        add(add(mul(us, x[1]), mul(u, q)), p),
        add(mul(v, q), mul(us, x[2])),
        add(mul(w, q), mul(us, x[3])),
        add(add(mul(h, q), mul(us, x[4])), mul(u, p)),
    ]


def jacobian_columns(cell, sign):
    u, v, w, k, h = cell
    shift = sign * DISS
    us = u + shift
    gk = 0.4 * k
    gv, gw = -0.4 * v, -0.4 * w
    return [
        [shift, gk - u * u, -(u * v), -(u * w), u * (gk - h)],
        [1.0, 1.6 * u + shift, v, w, h - 0.4 * (u * u)],
        [None, gv, us, None, u * gv],
        [None, gw, None, us, u * gw],
        [None, 0.4, None, None, 1.4 * u + shift],
    ]


def product(left, left_sign, right, right_sign):
    columns = [apply_jacobian(left, left_sign, c) for c in jacobian_columns(right, right_sign)]
    return [[columns[j][i] for j in range(5)] for i in range(5)]


def full(x):
    if x is None:
        return jnp.zeros((8, 128), F32)
    if isinstance(x, float):
        return jnp.full((8, 128), x, F32)
    return x


def dot_row(row, matrix, j):
    total = row[0] * matrix[0][j]
    for i in range(1, 5):
        total = total + row[i] * matrix[i][j]
    return total


def dot_vec(row, x):
    total = row[0] * x[0]
    for i in range(1, 5):
        total = total + row[i] * x[i]
    return total


def factor(matrix):
    d = [[matrix[i][j] for j in PIVOTS] for i in PIVOTS]
    inverse = []
    low = [[None] * 5 for _ in range(5)]
    for k in range(5):
        inverse.append(1.0 / d[k][k])
        for i in range(k + 1, 5):
            low[i][k] = d[i][k] * inverse[k]
            for j in range(k + 1, 5):
                d[i][j] = d[i][j] - low[i][k] * d[k][j]
    return d, low, inverse


def solve(factors, column):
    d, low, inverse = factors
    b = [column[i] for i in PIVOTS]
    for k in range(5):
        for i in range(k + 1, 5):
            b[i] = b[i] - low[i][k] * b[k]
    for k in reversed(range(5)):
        total = b[k]
        for j in range(k + 1, 5):
            total = total - d[k][j] * b[j]
        b[k] = total * inverse[k]
    x = [None] * 5
    for at, i in enumerate(PIVOTS):
        x[i] = b[at]
    return x


def quarters(c, lane):
    odd = (lane & 32) != 0
    high = (lane & 64) != 0

    def swap(a, b, mask, shift):
        return (
            jnp.where(mask, pltpu.roll(b, shift, 1), a),
            jnp.where(mask, b, pltpu.roll(a, 128 - shift, 1)),
        )

    c0, c1 = swap(c[0], c[1], odd, 32)
    c2, c3 = swap(c[2], c[3], odd, 32)
    c0, c2 = swap(c0, c2, high, 64)
    c1, c3 = swap(c1, c3, high, 64)
    return [c0, c1, c2, c3]


def pack(values, ref, rows, lane):
    values = list(values)
    while len(values) % 4:
        values.append(values[-1])
    for g in range(len(values) // 4):
        out = quarters(values[4 * g : 4 * g + 4], lane)
        for t in range(4):
            ref[pl.ds(8 * t * rows + g, 8, stride=rows), :] = out[t]


def unpack(ref, rows, count, lane):
    values = []
    for g in range((count + 3) // 4):
        got = [ref[pl.ds(8 * t * rows + g, 8, stride=rows), :] for t in range(4)]
        values += quarters(got, lane)
    return values[:count]


def kernel(
    state_ref, next_ref, diff_ref,
    st, pr, fx, rr, fac, left, halo_send, halo_left, halo_right,
    send_a, recv_a, send_b, recv_b, send_c, recv_c, sys, sol, xs, lin,
    ssem_h, rsem_h, ssem_a, rsem_a, ssem_b, rsem_b, ssem_c, rsem_c,
):
    me = lax.axis_index("stream")
    mine = lax.axis_index("span")

    barrier = pltpu.get_barrier_semaphore()

    def greet(d, _):
        pl.semaphore_signal(
            barrier, inc=1, device_id={"stream": lax.rem(me + d, N)}, device_id_type=MESH
        )
        return 0

    lax.fori_loop(1, N, greet, 0)
    span_right = lax.rem(mine + 1, SPAN)
    span_left = lax.rem(mine + SPAN - 1, SPAN)
    for other in (span_left, span_right):
        pl.semaphore_signal(barrier, inc=1, device_id={"span": other}, device_id_type=MESH)

    lane = lax.broadcasted_iota(jnp.int32, (8, 128), 1)
    sub_row = lax.broadcasted_iota(jnp.int32, (8, 128), 0)

    for f in range(5):
        for half in range(2):
            st[pl.ds(1 + 8 * half, 8), f] = jnp.swapaxes(
                state_ref[f, :, pl.ds(8 * half, 8), :], 0, 1
            )
    for f in range(5):
        packed = st[1, f]
        for i in range(CX):
            moved = pltpu.roll(st[1 + i, f], (2 + 4 * i) % 128, 1)
            packed = jnp.where((lane >> 2) == i, moved, packed)
        halo_send[f] = packed

    pl.semaphore_wait(barrier, N - 1 + 2)

    halos = []
    for at, (src, dst, who) in enumerate(
        (
            (st.at[CX], st.at[0], {"stream": lax.rem(me + 1, N)}),
            (st.at[1], st.at[CX + 1], {"stream": lax.rem(me + N - 1, N)}),
            (halo_send, halo_left, {"span": span_right}),
            (halo_send, halo_right, {"span": span_left}),
        )
    ):
        copy = pltpu.make_async_remote_copy(
            src_ref=src, dst_ref=dst, send_sem=ssem_h.at[at], recv_sem=rsem_h.at[at],
            device_id=who, device_id_type=MESH,
        )
        copy.start()
        halos.append(copy)

    def prepare(i, _):
        s = [st[i, f] for f in range(5)]
        u, v, w, k, p, h = primitives(s)
        for at, value in enumerate((u, v, w, k, h)):
            pr[i, at] = value
        flux = [s[1], s[1] * u + p, s[2] * u, s[3] * u, u * (s[4] + p)]
        for f in range(5):
            fx[i, f] = flux[f]
        return 0

    lax.fori_loop(1, CX + 1, prepare, 0)

    for copy in halos:
        copy.wait_recv()
    prepare(0, 0)
    prepare(CX + 1, 0)

    has_low = jnp.where(me > 0, 1.0, 0.0).astype(F32)
    has_high = jnp.where(me < N - 1, 1.0, 0.0).astype(F32)

    rim = [jnp.where((lane & 2) == 0, halo_left[f], halo_right[f]) for f in range(5)]
    _, v, _, _, p, _ = primitives(rim)
    rim_flux = [rim[2], rim[1] * v, rim[2] * v + p, rim[3] * v, v * (rim[4] + p)]
    for f in range(5):
        for i in range(CX):
            xs[1 + i, f] = pltpu.roll(rim_flux[f], (254 - 4 * i) % 128, 1)

    def right_side(i, _):
        s = [st[i, f] for f in range(5)]
        u, v, w, k, h = (pr[i, at] for at in range(5))
        total = h * s[0]
        p = total - s[4]
        g = [s[2], s[1] * v, s[2] * v + p, s[3] * v, v * total]
        wall = [s[3], s[1] * w, s[2] * w, s[3] * w + p, w * total]
        low = jnp.where(i == 1, has_low, 1.0)
        high = jnp.where(i == CX, has_high, 1.0)
        for f in range(5):
            edge = xs[i, f]
            near = pltpu.roll(jnp.where(lane < 1, edge, g[f]), 127, 1) - pltpu.roll(
                jnp.where(lane >= 127, edge, g[f]), 1, 1
            )
            far = pltpu.roll(jnp.where(lane < 2, edge, g[f]), 126, 1) - pltpu.roll(
                jnp.where(lane >= 126, edge, g[f]), 2, 1
            )
            span = 8.0 * near - far
            mirrored = wall[f] if f == 3 else -wall[f]
            above = jnp.where(sub_row == 7, wall[f], pltpu.roll(wall[f], 7, 0))
            below = jnp.where(sub_row == 0, mirrored, pltpu.roll(wall[f], 1, 0))
            stream = fx[i + 1, f] * high - fx[i - 1, f] * low
            curve = st[i + 1, f] * high + st[i - 1, f] * low - 2.0 * s[f]
            rr[i, f] = (
                DISS * curve - stream - (1.0 / 384.0) * span - (1.0 / 64.0) * (above - below)
            )
        return 0

    lax.fori_loop(1, CX + 1, right_side, 0)

    def cell(i):
        return tuple(pr[i, at] for at in range(5))

    def source(i):
        return [rr[i, f] for f in range(5)]

    zero = jnp.zeros((8, 128), F32)
    one = jnp.ones((8, 128), F32)
    for i in range(5):
        for j in range(5):
            fac[0, 5 * i + j] = zero
            fac[0, 25 + 5 * i + j] = one if i == j else zero
        fac[0, 50 + i] = zero

    def eliminate(m, _):
        i = 2 * m + 2
        below2, below1, here, above1, above2 = (cell(i + t) for t in range(-2, 3))
        low = [[full(x) for x in row] for row in product(below1, 1.0, below2, 1.0)]
        upper = [[full(x) for x in row] for row in product(above1, -1.0, above2, -1.0)]
        first = product(below1, 1.0, here, -1.0)
        second = product(above1, -1.0, here, 1.0)
        r_low = apply_jacobian(below1, 1.0, source(i - 1))
        r_high = apply_jacobian(above1, -1.0, source(i + 1))
        r_here = source(i)
        f_before = [[fac[m, 5 * a + b] for b in range(5)] for a in range(5)]
        y_before = [fac[m, 50 + a] for a in range(5)]
        diag = []
        for a in range(5):
            row = []
            for b in range(5):
                value = full(add(first[a][b], second[a][b])) - dot_row(low[a], f_before, b)
                row.append(value + DIAG if a == b else value)
            diag.append(row)
        factors = factor(diag)
        column = [
            (1.0 / 25.6) * r_here[a] + (r_low[a] - r_high[a]) + dot_vec(low[a], y_before)
            for a in range(5)
        ]
        y = solve(factors, column)
        for a in range(5):
            fac[m + 1, 50 + a] = y[a]
        for b in range(5):
            x = solve(factors, [upper[a][b] for a in range(5)])
            for a in range(5):
                fac[m + 1, 5 * a + b] = x[a]
        s_before = [[fac[m, 25 + 5 * a + b] for b in range(5)] for a in range(5)]
        for b in range(5):
            x = solve(factors, [dot_row(low[a], s_before, b) for a in range(5)])
            for a in range(5):
                fac[m + 1, 25 + 5 * a + b] = x[a]
        return 0

    lax.fori_loop(0, 7, eliminate, 0)

    below2, below1, here = cell(CX - 2), cell(CX - 1), cell(CX)
    low = [[full(x) for x in row] for row in product(below1, 1.0, below2, 1.0)]
    own = product(below1, 1.0, here, -1.0)
    r_low = apply_jacobian(below1, 1.0, source(CX - 1))
    r_here = source(CX)
    f_last = [[fac[7, 5 * a + b] for b in range(5)] for a in range(5)]
    s_last = [[fac[7, 25 + 5 * a + b] for b in range(5)] for a in range(5)]
    y_last = [fac[7, 50 + a] for a in range(5)]
    to_low = [dot_row(low[a], s_last, b) for a in range(5) for b in range(5)]
    to_own = []
    for a in range(5):
        for b in range(5):
            value = full(own[a][b]) - dot_row(low[a], f_last, b)
            to_own.append(value + DIAG if a == b else value)
    to_source = [(1.0 / 25.6) * r_here[a] + r_low[a] + dot_vec(low[a], y_last) for a in range(5)]
    pack(to_low + to_own + to_source, send_a, ROWS, lane)

    def exchange(send, recv, ssem, rsem, rows):
        def copy_to(d):
            other = lax.rem(me + d, N)
            return pltpu.make_async_remote_copy(
                src_ref=send.at[pl.ds(pl.multiple_of(other * rows, rows), rows)],
                dst_ref=recv.at[pl.ds(pl.multiple_of(me * rows, rows), rows)],
                send_sem=ssem.at[d], recv_sem=rsem.at[d],
                device_id={"stream": other}, device_id_type=MESH,
            )

        def copy_from(d):
            other = lax.rem(me + N - d, N)
            return pltpu.make_async_remote_copy(
                src_ref=send.at[pl.ds(pl.multiple_of(me * rows, rows), rows)],
                dst_ref=recv.at[pl.ds(pl.multiple_of(other * rows, rows), rows)],
                send_sem=ssem.at[d], recv_sem=rsem.at[d],
                device_id={"stream": other}, device_id_type=MESH,
            )

        def start():
            def body(d, _):
                copy_to(d).start()
                return 0

            lax.fori_loop(1, N, body, 0)
            place = pl.ds(pl.multiple_of(me * rows, rows), rows)
            recv[place, :] = send[place, :]

        def wait_recv():
            def body(d, _):
                copy_from(d).wait_recv()
                return 0

            lax.fori_loop(1, N, body, 0)

        def wait_send():
            def body(d, _):
                copy_to(d).wait_send()
                return 0

            lax.fori_loop(1, N, body, 0)

        return start, wait_recv, wait_send

    start_a, arrived_a, sent_a = exchange(send_a, recv_a, ssem_a, rsem_a, ROWS)
    start_b, arrived_b, sent_b = exchange(send_b, recv_b, ssem_b, rsem_b, ROWS)
    start_c, arrived_c, sent_c = exchange(send_c, recv_c, ssem_c, rsem_c, BACK_ROWS)
    start_a()

    for copy in halos:
        copy.wait_send()

    outer, first, second = cell(0), cell(1), cell(2)
    diag = product(first, -1.0, outer, 1.0)
    upper = product(first, -1.0, second, -1.0)
    r_first = apply_jacobian(first, -1.0, source(1))
    for a in range(5):
        for b in range(5):
            left[5 * a + b] = full(upper[a][b])
            left[25 + 5 * a + b] = full(diag[a][b])
        left[50 + a] = -r_first[a]

    def follow(m, _):
        f_here = [[fac[m, 5 * a + b] for b in range(5)] for a in range(5)]
        s_here = [[fac[m, 25 + 5 * a + b] for b in range(5)] for a in range(5)]
        y_here = [fac[m, 50 + a] for a in range(5)]
        for a in range(5):
            row = [left[5 * a + b] for b in range(5)]
            for b in range(5):
                left[25 + 5 * a + b] = left[25 + 5 * a + b] - dot_row(row, s_here, b)
                left[5 * a + b] = dot_row(row, f_here, b)
            left[50 + a] = left[50 + a] + dot_vec(row, y_here)
        return 0

    lax.fori_loop(1, 8, follow, 0)
    pack([left[at] for at in range(55)], send_b, ROWS, lane)
    start_b()

    arrived_a()
    at_first = (sub_row == 0) & (lane < 32)
    at_last = (sub_row == 7) & (lane >= 96)
    values = unpack(recv_a, ROWS, 55, lane)
    for at in range(25):
        sys[at] = jnp.where(at_first, 0.0, values[at])
        sys[25 + at] = values[25 + at]
    for a in range(5):
        sys[75 + a] = values[50 + a]
    arrived_b()

    def after(x, d):
        if d >= 8:
            return pltpu.roll(x, 128 - 4 * d, 1)
        x = pltpu.roll(x, 8 - d, 0)
        return jnp.where(sub_row >= 8 - d, pltpu.roll(x, 96, 1), x)

    def before(x, d):
        if d >= 8:
            return pltpu.roll(x, 4 * d, 1)
        x = pltpu.roll(x, d, 0)
        return jnp.where(sub_row < d, pltpu.roll(x, 32, 1), x)

    values = unpack(recv_b, ROWS, 55, lane)
    values = [jnp.where(at_last, 0.0, after(x, 1)) for x in values]
    for at in range(25):
        sys[50 + at] = values[at]
        sys[25 + at] = sys[25 + at] + values[25 + at]
    for a in range(5):
        sys[75 + a] = sys[75 + a] + values[50 + a]

    for level in range(5):
        d = 1 << level
        factors = factor([[sys[25 + 5 * a + b] for b in range(5)] for a in range(5)])
        for b in range(5):
            x = solve(factors, [sys[5 * a + b] for a in range(5)])
            for a in range(5):
                sol[5 * a + b] = x[a]
            x = solve(factors, [sys[50 + 5 * a + b] for a in range(5)])
            for a in range(5):
                sol[25 + 5 * a + b] = x[a]
        x = solve(factors, [sys[75 + a] for a in range(5)])
        for a in range(5):
            sol[50 + a] = x[a]
        lows = [[sol[5 * a + b] for b in range(5)] for a in range(5)]
        ups = [[sol[25 + 5 * a + b] for b in range(5)] for a in range(5)]
        for b in range(5):
            low_column = [[before(sol[5 * a + b], d)] for a in range(5)]
            up_column = [[after(sol[25 + 5 * a + b], d)] for a in range(5)]
            cross_low = [[before(sol[25 + 5 * a + b], d)] for a in range(5)]
            cross_up = [[after(sol[5 * a + b], d)] for a in range(5)]
            for a in range(5):
                value = -(dot_row(lows[a], cross_low, 0) + dot_row(ups[a], cross_up, 0))
                sys[25 + 5 * a + b] = value + 1.0 if a == b else value
                if level < 4:
                    sys[5 * a + b] = dot_row(lows[a], low_column, 0)
                    sys[50 + 5 * a + b] = dot_row(ups[a], up_column, 0)
        r_low = [before(sol[50 + a], d) for a in range(5)]
        r_high = [after(sol[50 + a], d) for a in range(5)]
        for a in range(5):
            sys[75 + a] = sol[50 + a] + dot_vec(lows[a], r_low) + dot_vec(ups[a], r_high)
    factors = factor([[sys[25 + 5 * a + b] for b in range(5)] for a in range(5)])
    ends = solve(factors, [sys[75 + a] for a in range(5)])
    starts = [jnp.where(at_first, 0.0, before(x, 1)) for x in ends]
    pack(ends + starts, send_c, BACK_ROWS, lane)
    start_c()
    arrived_c()
    values = unpack(recv_c, BACK_ROWS, 10, lane)
    for f in range(5):
        xs[CX, f] = values[f]
        xs[0, f] = values[5 + f]

    def back(t, _):
        m = 7 - t
        x_left = [xs[0, f] for f in range(5)]
        x_right = [xs[2 * m + 2, f] for f in range(5)]
        for a in range(5):
            row_f = [fac[m, 5 * a + b] for b in range(5)]
            row_s = [fac[m, 25 + 5 * a + b] for b in range(5)]
            xs[2 * m, a] = fac[m, 50 + a] + (dot_vec(row_s, x_left) + dot_vec(row_f, x_right))
        return 0

    lax.fori_loop(0, 7, back, 0)

    def even(t, _):
        i = 2 * t + 1
        low_part = apply_jacobian(cell(i - 1), 1.0, [xs[i - 1, f] for f in range(5)])
        high_part = apply_jacobian(cell(i + 1), -1.0, [xs[i + 1, f] for f in range(5)])
        for f in range(5):
            xs[i, f] = 25.6 * (rr[i, f] + (low_part[f] - high_part[f]))
        return 0

    lax.fori_loop(0, 8, even, 0)

    def advance(i, _):
        new = [st[i, f] + xs[i, f] for f in range(5)]
        flux = apply_jacobian(cell(i), 0.0, new)
        for f in range(5):
            st[i, f] = new[f]
            lin[i, f] = flux[f]
        return 0

    held = apply_jacobian(cell(CX - 1), 1.0, [xs[CX - 1, f] for f in range(5)])
    t = [rr[CX, f] + held[f] - (1.25 / 32.0) * xs[CX, f] for f in range(5)]
    u, v, w, k, h = cell(CX + 1)
    z = u - DISS
    z_inv = 1.0 / z
    p0 = t[1] - (z + u) * t[0]
    x2 = (t[2] - v * t[0]) * z_inv
    x3 = (t[3] - w * t[0]) * z_inv
    x4 = (t[4] - h * t[0] - u * p0) * z_inv
    x0 = (p0 - 0.4 * (x4 - u * t[0] - v * x2 - w * x3)) / (0.4 * (h - k) - z * z)
    beyond = [x0, t[0] + DISS * x0, x2 + v * x0, x3 + w * x0, x4 + (h - u * z) * x0]
    base = apply_jacobian(cell(CX + 1), 0.0, [st[CX + 1, f] for f in range(5)])
    for f in range(5):
        lin[CX + 1, f] = has_high * (base[f] + (t[f] + DISS * beyond[f]))
    lax.fori_loop(0, CX + 1, advance, 0)
    for f in range(5):
        lin[0, f] = has_low * lin[0, f]

    def differ(i, _):
        for f in range(5):
            xs[i, f] = -0.5 * (lin[i + 1, f] - lin[i - 1, f])
        return 0

    lax.fori_loop(1, CX + 1, differ, 0)
    for f in range(5):
        for half in range(2):
            place = pl.ds(8 * half, 8)
            next_ref[f, :, place, :] = jnp.swapaxes(st[pl.ds(1 + 8 * half, 8), f], 0, 1)
            diff_ref[f, :, place, :] = jnp.swapaxes(xs[pl.ds(1 + 8 * half, 8), f], 0, 1)

    sent_a()
    sent_b()
    sent_c()


def on_device(state):
    def cells(*shape):
        return pltpu.VMEM(shape + (8, 128), F32)

    return pl.pallas_call(
        kernel,
        out_shape=(jax.ShapeDtypeStruct(state.shape, F32), jax.ShapeDtypeStruct(state.shape, F32)),
        in_specs=[pl.BlockSpec(memory_space=pltpu.VMEM)],
        out_specs=(pl.BlockSpec(memory_space=pltpu.VMEM), pl.BlockSpec(memory_space=pltpu.VMEM)),
        scratch_shapes=[
            cells(CX + 2, 5), cells(CX + 2, 5), cells(CX + 2, 5), cells(CX + 2, 5),
            cells(8, 55), cells(55), cells(5), cells(5), cells(5),
            pltpu.VMEM((N * ROWS, 128), F32), pltpu.VMEM((N * ROWS, 128), F32),
            pltpu.VMEM((N * ROWS, 128), F32), pltpu.VMEM((N * ROWS, 128), F32),
            pltpu.VMEM((N * BACK_ROWS, 128), F32), pltpu.VMEM((N * BACK_ROWS, 128), F32),
            cells(80), cells(55), cells(CX + 2, 5), cells(CX + 2, 5),
            pltpu.SemaphoreType.DMA((4,)), pltpu.SemaphoreType.DMA((4,)),
            pltpu.SemaphoreType.DMA((N,)), pltpu.SemaphoreType.DMA((N,)),
            pltpu.SemaphoreType.DMA((N,)), pltpu.SemaphoreType.DMA((N,)),
            pltpu.SemaphoreType.DMA((N,)), pltpu.SemaphoreType.DMA((N,)),
        ],
        compiler_params=pltpu.CompilerParams(
            collective_id=0, has_side_effects=True, vmem_limit_bytes=32 * 1024 * 1024
        ),
    )(state)


def solution(mesh):
    spec = P(None, None, "stream", "span")
    return jax.shard_map(
        on_device, mesh=mesh, in_specs=(spec,), out_specs=(spec, spec), check_vma=False
    )
```

```python
import jax
import jax.numpy as jnp
from jax import lax
from jax.experimental import pallas as pl
from jax.experimental.pallas import tpu as pltpu
from jax.sharding import PartitionSpec as P

MESH = pl.DeviceIdType.MESH
N = 32
SPAN = 8
CX = 16
DISS = 1.0 / 256.0
DIAG = 1.25 / 819.2
PIVOTS = (1, 2, 3, 0, 4)
MATRIX = (27, 32)
SOURCE = (3, 8)
BACK = (3, 8)
F32 = jnp.float32


def mul(a, b):
    if a is None or b is None:
        return None
    if isinstance(a, float) and a == 1.0:
        return b
    if isinstance(b, float) and b == 1.0:
        return a
    return a * b


def add(a, b):
    if a is None:
        return b
    if b is None:
        return a
    return a + b


def sub(a, b):
    if b is None:
        return a
    if a is None:
        return -b
    return a - b


def primitives(s):
    inv = 1.0 / s[0]
    u, v, w = s[1] * inv, s[2] * inv, s[3] * inv
    k = 0.5 * (u * u + v * v + w * w)
    p = 0.4 * (s[4] - s[0] * k)
    return u, v, w, k, p, (s[4] + p) * inv


def apply_jacobian(cell, sign, x):
    u, v, w, k, h = cell
    us = u + sign * DISS if sign else u
    q = sub(x[1], mul(u, x[0]))
    inner = sub(mul(k, x[0]), mul(u, x[1]))
    inner = sub(sub(inner, mul(v, x[2])), mul(w, x[3]))
    p = mul(0.4, add(inner, x[4]))
    top = x[1]
    if sign and x[0] is not None:
        top = add(top, mul(sign * DISS, x[0]))
    return [
        top,
        add(add(mul(us, x[1]), mul(u, q)), p),
        add(mul(v, q), mul(us, x[2])),
        add(mul(w, q), mul(us, x[3])),
        add(add(mul(h, q), mul(us, x[4])), mul(u, p)),
    ]


def jacobian_columns(cell, sign):
    u, v, w, k, h = cell
    shift = sign * DISS
    us = u + shift
    gk = 0.4 * k
    gv, gw = -0.4 * v, -0.4 * w
    return [
        [shift, gk - u * u, -(u * v), -(u * w), u * (gk - h)],
        [1.0, 1.6 * u + shift, v, w, h - 0.4 * (u * u)],
        [None, gv, us, None, u * gv],
        [None, gw, None, us, u * gw],
        [None, 0.4, None, None, 1.4 * u + shift],
    ]


def product(left, left_sign, right, right_sign):
    columns = [apply_jacobian(left, left_sign, c) for c in jacobian_columns(right, right_sign)]
    return [[columns[j][i] for j in range(5)] for i in range(5)]


def full(x):
    if x is None:
        return jnp.zeros((8, 128), F32)
    if isinstance(x, float):
        return jnp.full((8, 128), x, F32)
    return x


def times_jacobian(t, cell):
    u, v, w, k, h = cell
    us = u + DISS
    alpha = (t[1] * u + t[2] * v) + (t[3] * w + t[4] * h)
    beta = 0.4 * (t[1] + u * t[4])
    return [
        (beta * k - u * alpha) + DISS * t[0],
        (t[0] + us * t[1]) + (alpha - beta * u),
        us * t[2] - beta * v,
        us * t[3] - beta * w,
        us * t[4] + beta,
    ]


def dot_row(row, matrix, j):
    total = row[0] * matrix[0][j]
    for i in range(1, 5):
        total = total + row[i] * matrix[i][j]
    return total


def dot_vec(row, x):
    total = row[0] * x[0]
    for i in range(1, 5):
        total = total + row[i] * x[i]
    return total


def factor(matrix):
    d = [[matrix[i][j] for j in PIVOTS] for i in PIVOTS]
    inverse = []
    low = [[None] * 5 for _ in range(5)]
    for k in range(5):
        inverse.append(1.0 / d[k][k])
        for i in range(k + 1, 5):
            low[i][k] = d[i][k] * inverse[k]
            for j in range(k + 1, 5):
                d[i][j] = d[i][j] - low[i][k] * d[k][j]
    return d, low, inverse


def keep_factors(factors, ref, m):
    d, low, inverse = factors
    kept = [d[k][j] for k in range(5) for j in range(k + 1, 5)]
    kept += [low[i][k] for k in range(5) for i in range(k + 1, 5)] + inverse
    for at, value in enumerate(kept):
        ref[m, at] = value


def kept_factors(ref, m):
    d, low = [[None] * 5 for _ in range(5)], [[None] * 5 for _ in range(5)]
    at = 0
    for k in range(5):
        for j in range(k + 1, 5):
            d[k][j] = ref[m, at]
            low[j][k] = ref[m, at + 10]
            at += 1
    return d, low, [ref[m, 20 + k] for k in range(5)]


def solve(factors, column):
    d, low, inverse = factors
    b = [column[i] for i in PIVOTS]
    for k in range(5):
        for i in range(k + 1, 5):
            b[i] = b[i] - low[i][k] * b[k]
    for k in reversed(range(5)):
        total = b[k]
        for j in range(k + 1, 5):
            total = total - d[k][j] * b[j]
        b[k] = total * inverse[k]
    x = [None] * 5
    for at, i in enumerate(PIVOTS):
        x[i] = b[at]
    return x


def quarters(c, lane):
    odd = (lane & 32) != 0
    high = (lane & 64) != 0

    def swap(a, b, mask, shift):
        return (
            jnp.where(mask, pltpu.roll(b, shift, 1), a),
            jnp.where(mask, b, pltpu.roll(a, 128 - shift, 1)),
        )

    c0, c1 = swap(c[0], c[1], odd, 32)
    c2, c3 = swap(c[2], c[3], odd, 32)
    c0, c2 = swap(c0, c2, high, 64)
    c1, c3 = swap(c1, c3, high, 64)
    return [c0, c1, c2, c3]


def pack(values, ref, rows, lane, first=0):
    values = list(values)
    rows = rows[1]
    while len(values) % 4:
        values.append(values[-1])
    for g in range(len(values) // 4):
        out = quarters(values[4 * g : 4 * g + 4], lane)
        for t in range(4):
            ref[pl.ds(8 * t * rows + first + g, 8, stride=rows), :] = out[t]


def unpack(ref, rows, count, lane):
    values = []
    rows = rows[1]
    for g in range((count + 3) // 4):
        got = [ref[pl.ds(8 * t * rows + g, 8, stride=rows), :] for t in range(4)]
        values += quarters(got, lane)
    return values[:count]


def kernel(
    state_ref, next_ref, diff_ref,
    here, st, pr, fx, rr, fac, ys, fct, lows, left, halo_send, halo_left, halo_right,
    send_a, recv_a, send_b, recv_b, send_c, recv_c, sys, sol, xs, lin,
    sem_in, ssem_h, rsem_h, ssem_x, rsem_x,
):
    me = lax.axis_index("stream")
    mine = lax.axis_index("span")
    span_right = lax.rem(mine + 1, SPAN)
    span_left = lax.rem(mine + SPAN - 1, SPAN)

    barrier = pltpu.get_barrier_semaphore()
    load = pltpu.make_async_copy(state_ref, here, sem_in)
    load.start()
    for other in (span_left, span_right):
        pl.semaphore_signal(barrier, inc=1, device_id={"span": other}, device_id_type=MESH)

    def greet(d, _):
        pl.semaphore_signal(
            barrier, inc=1, device_id={"stream": lax.rem(me + d, N)}, device_id_type=MESH
        )
        return 0

    lax.fori_loop(1, N, greet, 0)
    load.wait()

    lane = lax.broadcasted_iota(jnp.int32, (8, 128), 1)
    sub_row = lax.broadcasted_iota(jnp.int32, (8, 128), 0)

    for f in range(5):
        for half in range(2):
            st[pl.ds(1 + 8 * half, 8), f] = jnp.swapaxes(here[f, :, pl.ds(8 * half, 8), :], 0, 1)

    def prepare(i, _):
        s = [st[i, f] for f in range(5)]
        u, v, w, k, p, h = primitives(s)
        for at, value in enumerate((u, v, w, k, h)):
            pr[i, at] = value
        flux = [s[1], s[1] * u + p, s[2] * u, s[3] * u, u * (s[4] + p)]
        for f in range(5):
            fx[i, f] = flux[f]
        return 0

    lax.fori_loop(1, CX + 1, prepare, 0)

    def cell(i):
        return tuple(pr[i, at] for at in range(5))

    def eliminate(m, first_node):
        i = 2 * m + 2
        below1, middle, above1, above2 = (cell(i + t) for t in range(-1, 3))
        upper = [[full(x) for x in row] for row in product(above1, -1.0, above2, -1.0)]
        first = product(below1, 1.0, middle, -1.0)
        second = product(above1, -1.0, middle, 1.0)
        diag = [[full(add(first[a][b], second[a][b])) for b in range(5)] for a in range(5)]
        if first_node:
            columns = jacobian_columns(below1, 1.0)
            spike = [[full(columns[b][a]) for b in range(5)] for a in range(5)]
        else:
            low = [[full(x) for x in row] for row in product(below1, 1.0, cell(i - 2), 1.0)]
            f_before = [[fac[m - 1, 5 * a + b] for b in range(5)] for a in range(5)]
            for a in range(5):
                for b in range(5):
                    lows[m, 5 * a + b] = low[a][b]
                    diag[a][b] = diag[a][b] - dot_row(low[a], f_before, b)
        for a in range(5):
            diag[a][a] = diag[a][a] + DIAG
        factors = factor(diag)
        keep_factors(factors, fct, m)
        for b in range(5):
            x = solve(factors, [upper[a][b] for a in range(5)])
            for a in range(5):
                fac[m, 5 * a + b] = x[a]
        if not first_node:
            s_before = [[fac[m - 1, 25 + 5 * a + b] for b in range(5)] for a in range(5)]
            spike = [[dot_row(low[a], s_before, b) for b in range(5)] for a in range(5)]
        for b in range(5):
            x = solve(factors, [spike[a][b] for a in range(5)])
            for a in range(5):
                fac[m, 25 + 5 * a + b] = x[a]

    def eliminate_step(m, _):
        eliminate(m, False)
        return 0

    eliminate(0, True)
    lax.fori_loop(1, 7, eliminate_step, 0)

    low = [[full(x) for x in row] for row in product(cell(CX - 1), 1.0, cell(CX - 2), 1.0)]
    own = product(cell(CX - 1), 1.0, cell(CX), -1.0)
    f_last = [[fac[6, 5 * a + b] for b in range(5)] for a in range(5)]
    s_last = [[fac[6, 25 + 5 * a + b] for b in range(5)] for a in range(5)]
    to_low = [dot_row(low[a], s_last, b) for a in range(5) for b in range(5)]
    to_own = []
    for a in range(5):
        for b in range(5):
            lows[7, 5 * a + b] = low[a][b]
            value = full(own[a][b]) - dot_row(low[a], f_last, b)
            to_own.append(value + DIAG if a == b else value)
    pack((to_low + to_own)[:48], send_a, MATRIX, lane)

    upper = product(cell(1), -1.0, cell(2), -1.0)
    columns = jacobian_columns(cell(1), -1.0)
    for a in range(5):
        for b in range(5):
            left[0, 5 * a + b] = full(upper[a][b])
            left[0, 25 + 5 * a + b] = full(columns[b][a])

    def follow(m, _):
        f_here = [[fac[m, 5 * a + b] for b in range(5)] for a in range(5)]
        s_here = [[fac[m, 25 + 5 * a + b] for b in range(5)] for a in range(5)]
        for a in range(5):
            row = [left[m, 5 * a + b] for b in range(5)]
            for b in range(5):
                left[m + 1, 25 + 5 * a + b] = left[m, 25 + 5 * a + b] - dot_row(row, s_here, b)
                left[m + 1, 5 * a + b] = dot_row(row, f_here, b)
        return 0

    lax.fori_loop(0, 7, follow, 0)
    rest = to_own[-2:] + [left[7, at] for at in range(50)] + list(cell(CX))
    pack(rest, send_a, MATRIX, lane, 12)

    for f in range(5):
        packed = st[1, f]
        for i in range(CX):
            moved = pltpu.roll(st[1 + i, f], (2 + 4 * i) % 128, 1)
            packed = jnp.where((lane >> 2) == i, moved, packed)
        halo_send[f] = packed

    pl.semaphore_wait(barrier, N - 1 + 2)

    halos = []
    for at, (src, dst, who) in enumerate(
        (
            (st.at[CX], st.at[0], {"stream": lax.rem(me + 1, N)}),
            (st.at[1], st.at[CX + 1], {"stream": lax.rem(me + N - 1, N)}),
            (halo_send, halo_left, {"span": span_right}),
            (halo_send, halo_right, {"span": span_left}),
        )
    ):
        copy = pltpu.make_async_remote_copy(
            src_ref=src, dst_ref=dst, send_sem=ssem_h.at[at], recv_sem=rsem_h.at[at],
            device_id=who, device_id_type=MESH,
        )
        copy.start()
        halos.append(copy)

    def exchange(send, recv, at, rows):
        count, stride = rows

        def start():
            def body(d, _):
                other = lax.rem(me + d, N)
                pltpu.make_async_remote_copy(
                    src_ref=send.at[pl.ds(pl.multiple_of(other * stride, 8), count)],
                    dst_ref=recv.at[pl.ds(pl.multiple_of(me * stride, 8), count)],
                    send_sem=ssem_x.at[at], recv_sem=rsem_x.at[at],
                    device_id={"stream": other}, device_id_type=MESH,
                ).start()
                return 0

            lax.fori_loop(1, N, body, 0)
            place = pl.ds(pl.multiple_of(me * stride, 8), stride)
            recv[place, :] = send[place, :]

        everything = pltpu.make_async_remote_copy(
            src_ref=send.at[pl.ds(0, (N - 1) * count)],
            dst_ref=recv.at[pl.ds(0, (N - 1) * count)],
            send_sem=ssem_x.at[at], recv_sem=rsem_x.at[at],
            device_id={"stream": lax.rem(me + 1, N)}, device_id_type=MESH,
        )
        return start, everything.wait_recv, everything.wait_send

    start_a, arrived_a, sent_a = exchange(send_a, recv_a, 0, MATRIX)
    start_b, arrived_b, sent_b = exchange(send_b, recv_b, 1, SOURCE)
    start_c, arrived_c, sent_c = exchange(send_c, recv_c, 2, BACK)
    start_a()

    for copy in halos:
        copy.wait_recv()
    prepare(0, 0)
    prepare(CX + 1, 0)

    has_low = jnp.where(me > 0, 1.0, 0.0).astype(F32)
    has_high = jnp.where(me < N - 1, 1.0, 0.0).astype(F32)

    rim = [jnp.where((lane & 2) == 0, halo_left[f], halo_right[f]) for f in range(5)]
    _, v, _, _, p, _ = primitives(rim)
    rim_flux = [rim[2], rim[1] * v, rim[2] * v + p, rim[3] * v, v * (rim[4] + p)]
    for f in range(5):
        for i in range(CX):
            xs[1 + i, f] = pltpu.roll(rim_flux[f], (254 - 4 * i) % 128, 1)

    def right_side(i, _):
        s = [st[i, f] for f in range(5)]
        u, v, w, k, h = (pr[i, at] for at in range(5))
        total = h * s[0]
        p = total - s[4]
        g = [s[2], s[1] * v, s[2] * v + p, s[3] * v, v * total]
        wall = [s[3], s[1] * w, s[2] * w, s[3] * w + p, w * total]
        low = jnp.where(i == 1, has_low, 1.0)
        high = jnp.where(i == CX, has_high, 1.0)
        for f in range(5):
            edge = xs[i, f]
            near = pltpu.roll(jnp.where(lane < 1, edge, g[f]), 127, 1) - pltpu.roll(
                jnp.where(lane >= 127, edge, g[f]), 1, 1
            )
            far = pltpu.roll(jnp.where(lane < 2, edge, g[f]), 126, 1) - pltpu.roll(
                jnp.where(lane >= 126, edge, g[f]), 2, 1
            )
            span = 8.0 * near - far
            mirrored = wall[f] if f == 3 else -wall[f]
            above = jnp.where(sub_row == 7, wall[f], pltpu.roll(wall[f], 7, 0))
            below = jnp.where(sub_row == 0, mirrored, pltpu.roll(wall[f], 1, 0))
            stream = fx[i + 1, f] * high - fx[i - 1, f] * low
            curve = st[i + 1, f] * high + st[i - 1, f] * low - 2.0 * s[f]
            rr[i, f] = (
                DISS * curve - stream - (1.0 / 384.0) * span - (1.0 / 64.0) * (above - below)
            )
        return 0

    lax.fori_loop(1, CX + 1, right_side, 0)

    def source(i):
        return [rr[i, f] for f in range(5)]

    y = None
    r_first = apply_jacobian(cell(1), -1.0, source(1))
    to_left = [-r_first[a] for a in range(5)]
    for m in range(8):
        i = 2 * m + 2
        r_here = source(i)
        r_low = apply_jacobian(cell(i - 1), 1.0, source(i - 1))
        column = [(1.0 / 25.6) * r_here[a] + r_low[a] for a in range(5)]
        if m < 7:
            r_high = apply_jacobian(cell(i + 1), -1.0, source(i + 1))
            column = [column[a] - r_high[a] for a in range(5)]
        if m > 0:
            column = [
                column[a] + dot_vec([lows[m, 5 * a + b] for b in range(5)], y) for a in range(5)
            ]
        if m < 7:
            y = solve(kept_factors(fct, m), column)
            for a in range(5):
                ys[m, a] = y[a]
                row = [left[m, 5 * a + b] for b in range(5)]
                to_left[a] = to_left[a] + dot_vec(row, y)
    pack(column + to_left, send_b, SOURCE, lane)
    start_b()

    at_first = (sub_row == 0) & (lane < 32)
    at_last = (sub_row == 7) & (lane >= 96)

    def after(x, d):
        if d >= 8:
            return pltpu.roll(x, 128 - 4 * d, 1)
        x = pltpu.roll(x, 8 - d, 0)
        return jnp.where(sub_row >= 8 - d, pltpu.roll(x, 96, 1), x)

    def before(x, d):
        if d >= 8:
            return pltpu.roll(x, 4 * d, 1)
        x = pltpu.roll(x, d, 0)
        return jnp.where(sub_row < d, pltpu.roll(x, 32, 1), x)

    arrived_a()
    values = unpack(recv_a, MATRIX, 105, lane)
    last_cell = values[100:]
    cell_before = [before(x, 1) for x in last_cell]
    for a in range(5):
        low = times_jacobian(values[5 * a : 5 * a + 5], cell_before)
        share = [jnp.where(at_last, 0.0, after(values[75 + 5 * a + b], 1)) for b in range(5)]
        share = times_jacobian(share, last_cell)
        for b in range(5):
            sys[5 * a + b] = jnp.where(at_first, 0.0, low[b])
            sys[25 + 5 * a + b] = values[25 + 5 * a + b] + share[b]
            sys[50 + 5 * a + b] = jnp.where(at_last, 0.0, after(values[50 + 5 * a + b], 1))
    arrived_b()
    values = unpack(recv_b, SOURCE, 10, lane)
    for a in range(5):
        sys[75 + a] = values[a] + jnp.where(at_last, 0.0, after(values[5 + a], 1))

    for level in range(5):
        d = 1 << level
        factors = factor([[sys[25 + 5 * a + b] for b in range(5)] for a in range(5)])
        for b in range(5):
            x = solve(factors, [sys[5 * a + b] for a in range(5)])
            for a in range(5):
                sol[5 * a + b] = x[a]
            x = solve(factors, [sys[50 + 5 * a + b] for a in range(5)])
            for a in range(5):
                sol[25 + 5 * a + b] = x[a]
        x = solve(factors, [sys[75 + a] for a in range(5)])
        for a in range(5):
            sol[50 + a] = x[a]
        lows = [[sol[5 * a + b] for b in range(5)] for a in range(5)]
        ups = [[sol[25 + 5 * a + b] for b in range(5)] for a in range(5)]
        for b in range(5):
            low_column = [[before(sol[5 * a + b], d)] for a in range(5)]
            up_column = [[after(sol[25 + 5 * a + b], d)] for a in range(5)]
            cross_low = [[before(sol[25 + 5 * a + b], d)] for a in range(5)]
            cross_up = [[after(sol[5 * a + b], d)] for a in range(5)]
            for a in range(5):
                value = -(dot_row(lows[a], cross_low, 0) + dot_row(ups[a], cross_up, 0))
                sys[25 + 5 * a + b] = value + 1.0 if a == b else value
                if level < 4:
                    sys[5 * a + b] = dot_row(lows[a], low_column, 0)
                    sys[50 + 5 * a + b] = dot_row(ups[a], up_column, 0)
        r_low = [before(sol[50 + a], d) for a in range(5)]
        r_high = [after(sol[50 + a], d) for a in range(5)]
        for a in range(5):
            sys[75 + a] = sol[50 + a] + dot_vec(lows[a], r_low) + dot_vec(ups[a], r_high)
    factors = factor([[sys[25 + 5 * a + b] for b in range(5)] for a in range(5)])
    ends = solve(factors, [sys[75 + a] for a in range(5)])
    starts = [jnp.where(at_first, 0.0, before(x, 1)) for x in ends]
    pack(ends + starts, send_c, BACK, lane)
    start_c()
    arrived_c()
    values = unpack(recv_c, BACK, 10, lane)
    for f in range(5):
        xs[CX, f] = values[f]
        xs[0, f] = values[5 + f]

    g = apply_jacobian(cell(0), 1.0, [xs[0, f] for f in range(5)])
    x_right = [xs[CX, f] for f in range(5)]
    for m in reversed(range(7)):
        x_here = []
        for a in range(5):
            row_f = [fac[m, 5 * a + b] for b in range(5)]
            row_s = [fac[m, 25 + 5 * a + b] for b in range(5)]
            x_here.append((ys[m, a] + dot_vec(row_s, g)) + dot_vec(row_f, x_right))
            xs[2 * m + 2, a] = x_here[a]
        x_right = x_here

    def even(t, _):
        i = 2 * t + 1
        low_part = apply_jacobian(cell(i - 1), 1.0, [xs[i - 1, f] for f in range(5)])
        high_part = apply_jacobian(cell(i + 1), -1.0, [xs[i + 1, f] for f in range(5)])
        for f in range(5):
            xs[i, f] = 25.6 * (rr[i, f] + (low_part[f] - high_part[f]))
        return 0

    lax.fori_loop(0, 8, even, 0)

    def advance(i, _):
        new = [st[i, f] + xs[i, f] for f in range(5)]
        flux = apply_jacobian(cell(i), 0.0, new)
        for f in range(5):
            st[i, f] = new[f]
            lin[i, f] = flux[f]
        return 0

    for copy in halos:
        copy.wait_send()

    held = apply_jacobian(cell(CX - 1), 1.0, [xs[CX - 1, f] for f in range(5)])
    t = [rr[CX, f] + held[f] - (1.25 / 32.0) * xs[CX, f] for f in range(5)]
    u, v, w, k, h = cell(CX + 1)
    z = u - DISS
    z_inv = 1.0 / z
    p0 = t[1] - (z + u) * t[0]
    x2 = (t[2] - v * t[0]) * z_inv
    x3 = (t[3] - w * t[0]) * z_inv
    x4 = (t[4] - h * t[0] - u * p0) * z_inv
    x0 = (p0 - 0.4 * (x4 - u * t[0] - v * x2 - w * x3)) / (0.4 * (h - k) - z * z)
    beyond = [x0, t[0] + DISS * x0, x2 + v * x0, x3 + w * x0, x4 + (h - u * z) * x0]
    base = apply_jacobian(cell(CX + 1), 0.0, [st[CX + 1, f] for f in range(5)])
    for f in range(5):
        lin[CX + 1, f] = has_high * (base[f] + (t[f] + DISS * beyond[f]))
    lax.fori_loop(0, CX + 1, advance, 0)
    for f in range(5):
        lin[0, f] = has_low * lin[0, f]

    def differ(i, _):
        for f in range(5):
            xs[i, f] = -0.5 * (lin[i + 1, f] - lin[i - 1, f])
        return 0

    lax.fori_loop(1, CX + 1, differ, 0)
    for f in range(5):
        for half in range(2):
            place = pl.ds(8 * half, 8)
            next_ref[f, :, place, :] = jnp.swapaxes(st[pl.ds(1 + 8 * half, 8), f], 0, 1)
            diff_ref[f, :, place, :] = jnp.swapaxes(xs[pl.ds(1 + 8 * half, 8), f], 0, 1)

    sent_a()
    sent_b()
    sent_c()


def on_device(state):
    def cells(*shape):
        return pltpu.VMEM(shape + (8, 128), F32)

    return pl.pallas_call(
        kernel,
        out_shape=(jax.ShapeDtypeStruct(state.shape, F32), jax.ShapeDtypeStruct(state.shape, F32)),
        in_specs=[pl.BlockSpec(memory_space=pl.ANY)],
        out_specs=(pl.BlockSpec(memory_space=pltpu.VMEM), pl.BlockSpec(memory_space=pltpu.VMEM)),
        scratch_shapes=[
            pltpu.VMEM(state.shape, F32),
            cells(CX + 2, 5), cells(CX + 2, 5), cells(CX + 2, 5), cells(CX + 2, 5),
            cells(7, 50), cells(7, 5), cells(7, 30), cells(8, 25), cells(8, 50),
            cells(5), cells(5), cells(5),
            pltpu.VMEM((N * MATRIX[1], 128), F32), pltpu.VMEM((N * MATRIX[1], 128), F32),
            pltpu.VMEM((N * SOURCE[1], 128), F32), pltpu.VMEM((N * SOURCE[1], 128), F32),
            pltpu.VMEM((N * BACK[1], 128), F32), pltpu.VMEM((N * BACK[1], 128), F32),
            cells(80), cells(55), cells(CX + 2, 5), cells(CX + 2, 5),
            pltpu.SemaphoreType.DMA, pltpu.SemaphoreType.DMA((4,)), pltpu.SemaphoreType.DMA((4,)),
            pltpu.SemaphoreType.DMA((3,)), pltpu.SemaphoreType.DMA((3,)),
        ],
        compiler_params=pltpu.CompilerParams(
            collective_id=0, has_side_effects=True, vmem_limit_bytes=56 * 1024 * 1024
        ),
    )(state)


def solution(mesh):
    spec = P(None, None, "stream", "span")
    return jax.shard_map(
        on_device, mesh=mesh, in_specs=(spec,), out_specs=(spec, spec), check_vma=False
    )
```

```python
import jax
import jax.numpy as jnp
from jax import lax
from jax.experimental import pallas as pl
from jax.experimental.pallas import tpu as pltpu
from jax.sharding import PartitionSpec as P

MESH = pl.DeviceIdType.MESH
N = 32
SPAN = 8
CX = 16
DISS = 1.0 / 256.0
DIAG = 1.25 / 819.2
PIVOTS = (1, 2, 3, 0, 4)
OWN = (14, 16)
SHARE = (13, 16)
SOURCE = (3, 8)
BACK = (3, 8)
F32 = jnp.float32


STEPS = [(dx, dz) for dz in (4, 3, 5, 2, 6, 1, 7, 0) for dx in (2, 1, 3, 0) if dx or dz]


def mul(a, b):
    if a is None or b is None:
        return None
    if isinstance(a, float) and a == 1.0:
        return b
    if isinstance(b, float) and b == 1.0:
        return a
    return a * b


def add(a, b):
    if a is None:
        return b
    if b is None:
        return a
    return a + b


def sub(a, b):
    if b is None:
        return a
    if a is None:
        return -b
    return a - b


def primitives(s):
    inv = 1.0 / s[0]
    u, v, w = s[1] * inv, s[2] * inv, s[3] * inv
    k = 0.5 * (u * u + v * v + w * w)
    p = 0.4 * (s[4] - s[0] * k)
    return u, v, w, k, p, (s[4] + p) * inv


def apply_jacobian(cell, sign, x):
    u, v, w, k, h = cell
    us = u + sign * DISS if sign else u
    q = sub(x[1], mul(u, x[0]))
    inner = sub(mul(k, x[0]), mul(u, x[1]))
    inner = sub(sub(inner, mul(v, x[2])), mul(w, x[3]))
    p = mul(0.4, add(inner, x[4]))
    top = x[1]
    if sign and x[0] is not None:
        top = add(top, mul(sign * DISS, x[0]))
    return [
        top,
        add(add(mul(us, x[1]), mul(u, q)), p),
        add(mul(v, q), mul(us, x[2])),
        add(mul(w, q), mul(us, x[3])),
        add(add(mul(h, q), mul(us, x[4])), mul(u, p)),
    ]


def jacobian_columns(cell, sign):
    u, v, w, k, h = cell
    shift = sign * DISS
    us = u + shift
    gk = 0.4 * k
    gv, gw = -0.4 * v, -0.4 * w
    return [
        [shift, gk - u * u, -(u * v), -(u * w), u * (gk - h)],
        [1.0, 1.6 * u + shift, v, w, h - 0.4 * (u * u)],
        [None, gv, us, None, u * gv],
        [None, gw, None, us, u * gw],
        [None, 0.4, None, None, 1.4 * u + shift],
    ]


def product(left, left_sign, right, right_sign):
    columns = [apply_jacobian(left, left_sign, c) for c in jacobian_columns(right, right_sign)]
    return [[columns[j][i] for j in range(5)] for i in range(5)]


def full(x):
    if x is None:
        return jnp.zeros((8, 128), F32)
    if isinstance(x, float):
        return jnp.full((8, 128), x, F32)
    return x


def times_jacobian(t, cell):
    u, v, w, k, h = cell
    us = u + DISS
    alpha = (t[1] * u + t[2] * v) + (t[3] * w + t[4] * h)
    beta = 0.4 * (t[1] + u * t[4])
    return [
        (beta * k - u * alpha) + DISS * t[0],
        (t[0] + us * t[1]) + (alpha - beta * u),
        us * t[2] - beta * v,
        us * t[3] - beta * w,
        us * t[4] + beta,
    ]


def dot_row(row, matrix, j):
    total = row[0] * matrix[0][j]
    for i in range(1, 5):
        total = total + row[i] * matrix[i][j]
    return total


def dot_vec(row, x):
    total = row[0] * x[0]
    for i in range(1, 5):
        total = total + row[i] * x[i]
    return total


def factor(matrix):
    d = [[matrix[i][j] for j in PIVOTS] for i in PIVOTS]
    inverse = []
    low = [[None] * 5 for _ in range(5)]
    for k in range(5):
        inverse.append(1.0 / d[k][k])
        for i in range(k + 1, 5):
            low[i][k] = d[i][k] * inverse[k]
            for j in range(k + 1, 5):
                d[i][j] = d[i][j] - low[i][k] * d[k][j]
    return d, low, inverse


def keep_factors(factors, ref, m):
    d, low, inverse = factors
    kept = [d[k][j] for k in range(5) for j in range(k + 1, 5)]
    kept += [low[i][k] for k in range(5) for i in range(k + 1, 5)] + inverse
    for at, value in enumerate(kept):
        ref[m, at] = value


def kept_factors(ref, m):
    d, low = [[None] * 5 for _ in range(5)], [[None] * 5 for _ in range(5)]
    at = 0
    for k in range(5):
        for j in range(k + 1, 5):
            d[k][j] = ref[m, at]
            low[j][k] = ref[m, at + 10]
            at += 1
    return d, low, [ref[m, 20 + k] for k in range(5)]


def solve(factors, column):
    d, low, inverse = factors
    b = [column[i] for i in PIVOTS]
    for k in range(5):
        for i in range(k + 1, 5):
            b[i] = b[i] - low[i][k] * b[k]
    for k in reversed(range(5)):
        total = b[k]
        for j in range(k + 1, 5):
            total = total - d[k][j] * b[j]
        b[k] = total * inverse[k]
    x = [None] * 5
    for at, i in enumerate(PIVOTS):
        x[i] = b[at]
    return x


def quarters(c, lane):
    odd = (lane & 32) != 0
    high = (lane & 64) != 0

    def swap(a, b, mask, shift):
        return (
            jnp.where(mask, pltpu.roll(b, shift, 1), a),
            jnp.where(mask, b, pltpu.roll(a, 128 - shift, 1)),
        )

    c0, c1 = swap(c[0], c[1], odd, 32)
    c2, c3 = swap(c[2], c[3], odd, 32)
    c0, c2 = swap(c0, c2, high, 64)
    c1, c3 = swap(c1, c3, high, 64)
    return [c0, c1, c2, c3]


def pack(values, ref, rows, lane, first=0):
    values = list(values)
    rows = rows[1]
    while len(values) % 4:
        values.append(values[-1])
    for g in range(len(values) // 4):
        out = quarters(values[4 * g : 4 * g + 4], lane)
        for t in range(4):
            ref[pl.ds(8 * t * rows + first + g, 8, stride=rows), :] = out[t]


def unpack(ref, rows, count, lane):
    values = []
    rows = rows[1]
    for g in range((count + 3) // 4):
        got = [ref[pl.ds(8 * t * rows + g, 8, stride=rows), :] for t in range(4)]
        values += quarters(got, lane)
    return values[:count]


def kernel(
    here, next_ref, diff_ref,
    st, pr, fx, rr, fac, ys, fct, lows, left, halo_send, halo_left, halo_right,
    send_a, recv_a, send_b, recv_b, send_r, recv_r, send_c, recv_c, sys, sol, fct2, xs, lin,
    ssem_h, rsem_h, ssem_x, rsem_x,
):
    me = lax.axis_index("stream")
    mine = lax.axis_index("span")
    span_right = (mine + 1) & (SPAN - 1)
    span_left = (mine + SPAN - 1) & (SPAN - 1)

    barrier = pltpu.get_barrier_semaphore()

    def stepped(dx, dz):
        return (((me >> 3) + dx) & 3) * 8 + ((me + dz) & 7)

    for step in STEPS:
        pl.semaphore_signal(
            barrier, inc=1, device_id=(stepped(*step), mine), device_id_type=MESH
        )
    for other in (span_left, span_right):
        pl.semaphore_signal(barrier, inc=1, device_id={"span": other}, device_id_type=MESH)

    lane = lax.broadcasted_iota(jnp.int32, (8, 128), 1)
    sub_row = lax.broadcasted_iota(jnp.int32, (8, 128), 0)

    for f in range(5):
        for half in range(2):
            st[pl.ds(1 + 8 * half, 8), f] = jnp.swapaxes(here[f, :, pl.ds(8 * half, 8), :], 0, 1)

    def prepare(i, _):
        s = [st[i, f] for f in range(5)]
        u, v, w, k, p, h = primitives(s)
        for at, value in enumerate((u, v, w, k, h)):
            pr[i, at] = value
        flux = [s[1], s[1] * u + p, s[2] * u, s[3] * u, u * (s[4] + p)]
        for f in range(5):
            fx[i, f] = flux[f]
        return 0

    lax.fori_loop(1, CX + 1, prepare, 0)

    def cell(i):
        return tuple(pr[i, at] for at in range(5))

    def eliminate(m, first_node):
        i = 2 * m + 2
        below1, middle, above1, above2 = (cell(i + t) for t in range(-1, 3))
        upper = [[full(x) for x in row] for row in product(above1, -1.0, above2, -1.0)]
        first = product(below1, 1.0, middle, -1.0)
        second = product(above1, -1.0, middle, 1.0)
        diag = [[full(add(first[a][b], second[a][b])) for b in range(5)] for a in range(5)]
        if first_node:
            columns = jacobian_columns(below1, 1.0)
            spike = [[full(columns[b][a]) for b in range(5)] for a in range(5)]
        else:
            low = [[full(x) for x in row] for row in product(below1, 1.0, cell(i - 2), 1.0)]
            f_before = [[fac[m - 1, 5 * a + b] for b in range(5)] for a in range(5)]
            for a in range(5):
                for b in range(5):
                    lows[m, 5 * a + b] = low[a][b]
                    diag[a][b] = diag[a][b] - dot_row(low[a], f_before, b)
        for a in range(5):
            diag[a][a] = diag[a][a] + DIAG
        factors = factor(diag)
        keep_factors(factors, fct, m)
        for b in range(5):
            x = solve(factors, [upper[a][b] for a in range(5)])
            for a in range(5):
                fac[m, 5 * a + b] = x[a]
        if not first_node:
            s_before = [[fac[m - 1, 25 + 5 * a + b] for b in range(5)] for a in range(5)]
            spike = [[dot_row(low[a], s_before, b) for b in range(5)] for a in range(5)]
        for b in range(5):
            x = solve(factors, [spike[a][b] for a in range(5)])
            for a in range(5):
                fac[m, 25 + 5 * a + b] = x[a]

    def eliminate_step(m, _):
        eliminate(m, False)
        return 0

    eliminate(0, True)
    lax.fori_loop(1, 7, eliminate_step, 0)

    low = [[full(x) for x in row] for row in product(cell(CX - 1), 1.0, cell(CX - 2), 1.0)]
    own = product(cell(CX - 1), 1.0, cell(CX), -1.0)
    f_last = [[fac[6, 5 * a + b] for b in range(5)] for a in range(5)]
    s_last = [[fac[6, 25 + 5 * a + b] for b in range(5)] for a in range(5)]
    to_low = [dot_row(low[a], s_last, b) for a in range(5) for b in range(5)]
    to_own = []
    for a in range(5):
        for b in range(5):
            lows[7, 5 * a + b] = low[a][b]
            value = full(own[a][b]) - dot_row(low[a], f_last, b)
            to_own.append(value + DIAG if a == b else value)
    pack(to_low + to_own + list(cell(CX)), send_a, OWN, lane)

    for f in range(5):
        packed = st[1, f]
        for i in range(CX):
            moved = pltpu.roll(st[1 + i, f], (2 + 4 * i) % 128, 1)
            packed = jnp.where((lane >> 2) == i, moved, packed)
        halo_send[f] = packed

    pl.semaphore_wait(barrier, N - 1 + 2)

    halos = []
    for at, (src, dst, who) in enumerate(
        (
            (st.at[CX], st.at[0], {"stream": (me + 1) & (N - 1)}),
            (st.at[1], st.at[CX + 1], {"stream": (me + N - 1) & (N - 1)}),
            (halo_send, halo_left, {"span": span_right}),
            (halo_send, halo_right, {"span": span_left}),
        )
    ):
        copy = pltpu.make_async_remote_copy(
            src_ref=src, dst_ref=dst, send_sem=ssem_h.at[at], recv_sem=rsem_h.at[at],
            device_id=who, device_id_type=MESH,
        )
        copy.start()
        halos.append(copy)

    def exchange(send, recv, at, rows):
        count, stride = rows

        def start():
            def send_to(other):
                pltpu.make_async_remote_copy(
                    src_ref=send.at[pl.ds(pl.multiple_of(other * stride, 8), count)],
                    dst_ref=recv.at[pl.ds(pl.multiple_of(me * stride, 8), count)],
                    send_sem=ssem_x.at[at], recv_sem=rsem_x.at[at],
                    device_id=(other, mine), device_id_type=MESH,
                ).start()

            for step in STEPS:
                send_to(stepped(*step))
            place = pl.ds(pl.multiple_of(me * stride, 8), stride)
            recv[place, :] = send[place, :]

        everything = pltpu.make_async_remote_copy(
            src_ref=send.at[pl.ds(0, (N - 1) * count)],
            dst_ref=recv.at[pl.ds(0, (N - 1) * count)],
            send_sem=ssem_x.at[at], recv_sem=rsem_x.at[at],
            device_id=((me + 1) & (N - 1), mine), device_id_type=MESH,
        )
        return start, everything.wait_recv, everything.wait_send

    start_a, arrived_a, sent_a = exchange(send_a, recv_a, 0, OWN)
    start_b, arrived_b, sent_b = exchange(send_b, recv_b, 1, SHARE)
    start_r, arrived_r, sent_r = exchange(send_r, recv_r, 2, SOURCE)
    start_c, arrived_c, sent_c = exchange(send_c, recv_c, 3, BACK)
    start_a()

    upper = product(cell(1), -1.0, cell(2), -1.0)
    columns = jacobian_columns(cell(1), -1.0)
    for a in range(5):
        for b in range(5):
            left[0, 5 * a + b] = full(upper[a][b])
            left[0, 25 + 5 * a + b] = full(columns[b][a])

    def follow(m, _):
        f_here = [[fac[m, 5 * a + b] for b in range(5)] for a in range(5)]
        s_here = [[fac[m, 25 + 5 * a + b] for b in range(5)] for a in range(5)]
        for a in range(5):
            row = [left[m, 5 * a + b] for b in range(5)]
            for b in range(5):
                left[m + 1, 25 + 5 * a + b] = left[m, 25 + 5 * a + b] - dot_row(row, s_here, b)
                left[m + 1, 5 * a + b] = dot_row(row, f_here, b)
        return 0

    lax.fori_loop(0, 7, follow, 0)
    pack([left[7, at] for at in range(50)], send_b, SHARE, lane)
    start_b()

    for copy in halos:
        copy.wait_recv()
    prepare(0, 0)
    prepare(CX + 1, 0)

    has_low = jnp.where(me > 0, 1.0, 0.0).astype(F32)
    has_high = jnp.where(me < N - 1, 1.0, 0.0).astype(F32)

    rim = [jnp.where((lane & 2) == 0, halo_left[f], halo_right[f]) for f in range(5)]
    _, v, _, _, p, _ = primitives(rim)
    rim_flux = [rim[2], rim[1] * v, rim[2] * v + p, rim[3] * v, v * (rim[4] + p)]
    for f in range(5):
        for i in range(CX):
            xs[1 + i, f] = pltpu.roll(rim_flux[f], (254 - 4 * i) % 128, 1)

    def right_side(i, _):
        s = [st[i, f] for f in range(5)]
        u, v, w, k, h = (pr[i, at] for at in range(5))
        total = h * s[0]
        p = total - s[4]
        g = [s[2], s[1] * v, s[2] * v + p, s[3] * v, v * total]
        wall = [s[3], s[1] * w, s[2] * w, s[3] * w + p, w * total]
        low = jnp.where(i == 1, has_low, 1.0)
        high = jnp.where(i == CX, has_high, 1.0)
        for f in range(5):
            edge = xs[i, f]
            near = pltpu.roll(jnp.where(lane < 1, edge, g[f]), 127, 1) - pltpu.roll(
                jnp.where(lane >= 127, edge, g[f]), 1, 1
            )
            far = pltpu.roll(jnp.where(lane < 2, edge, g[f]), 126, 1) - pltpu.roll(
                jnp.where(lane >= 126, edge, g[f]), 2, 1
            )
            span = 8.0 * near - far
            mirrored = wall[f] if f == 3 else -wall[f]
            above = jnp.where(sub_row == 7, wall[f], pltpu.roll(wall[f], 7, 0))
            below = jnp.where(sub_row == 0, mirrored, pltpu.roll(wall[f], 1, 0))
            stream = fx[i + 1, f] * high - fx[i - 1, f] * low
            curve = st[i + 1, f] * high + st[i - 1, f] * low - 2.0 * s[f]
            rr[i, f] = (
                DISS * curve - stream - (1.0 / 384.0) * span - (1.0 / 64.0) * (above - below)
            )
        return 0

    lax.fori_loop(1, CX + 1, right_side, 0)

    def source(i):
        return [rr[i, f] for f in range(5)]

    y = None
    r_first = apply_jacobian(cell(1), -1.0, source(1))
    to_left = [-r_first[a] for a in range(5)]
    for m in range(8):
        i = 2 * m + 2
        r_here = source(i)
        r_low = apply_jacobian(cell(i - 1), 1.0, source(i - 1))
        column = [(1.0 / 25.6) * r_here[a] + r_low[a] for a in range(5)]
        if m < 7:
            r_high = apply_jacobian(cell(i + 1), -1.0, source(i + 1))
            column = [column[a] - r_high[a] for a in range(5)]
        if m > 0:
            column = [
                column[a] + dot_vec([lows[m, 5 * a + b] for b in range(5)], y) for a in range(5)
            ]
        if m < 7:
            y = solve(kept_factors(fct, m), column)
            for a in range(5):
                ys[m, a] = y[a]
                row = [left[m, 5 * a + b] for b in range(5)]
                to_left[a] = to_left[a] + dot_vec(row, y)
    pack(column + to_left, send_r, SOURCE, lane)
    start_r()

    at_first = (sub_row == 0) & (lane < 32)
    at_last = (sub_row == 7) & (lane >= 96)

    def after(x, d):
        if d >= 8:
            return pltpu.roll(x, 128 - 4 * d, 1)
        x = pltpu.roll(x, 8 - d, 0)
        return jnp.where(sub_row >= 8 - d, pltpu.roll(x, 96, 1), x)

    def before(x, d):
        if d >= 8:
            return pltpu.roll(x, 4 * d, 1)
        x = pltpu.roll(x, d, 0)
        return jnp.where(sub_row < d, pltpu.roll(x, 32, 1), x)

    arrived_a()
    values = unpack(recv_a, OWN, 55, lane)
    last_cell = values[50:]
    cell_before = [before(x, 1) for x in last_cell]
    for a in range(5):
        low = times_jacobian(values[5 * a : 5 * a + 5], cell_before)
        for b in range(5):
            sys[5 * a + b] = jnp.where(at_first, 0.0, low[b])
            sys[25 + 5 * a + b] = values[25 + 5 * a + b]
    arrived_b()
    values = unpack(recv_b, SHARE, 50, lane)
    for a in range(5):
        share = [jnp.where(at_last, 0.0, after(values[25 + 5 * a + b], 1)) for b in range(5)]
        share = times_jacobian(share, last_cell)
        for b in range(5):
            sys[25 + 5 * a + b] = sys[25 + 5 * a + b] + share[b]
            sys[50 + 5 * a + b] = jnp.where(at_last, 0.0, after(values[5 * a + b], 1))

    for level in range(5):
        d = 1 << level
        factors = factor([[sys[25 + 5 * a + b] for b in range(5)] for a in range(5)])
        keep_factors(factors, fct2, level)
        for b in range(5):
            x = solve(factors, [sys[5 * a + b] for a in range(5)])
            for a in range(5):
                sol[level, 5 * a + b] = x[a]
            x = solve(factors, [sys[50 + 5 * a + b] for a in range(5)])
            for a in range(5):
                sol[level, 25 + 5 * a + b] = x[a]
        low = [[sol[level, 5 * a + b] for b in range(5)] for a in range(5)]
        up = [[sol[level, 25 + 5 * a + b] for b in range(5)] for a in range(5)]
        for b in range(5):
            low_column = [[before(low[a][b], d)] for a in range(5)]
            up_column = [[after(up[a][b], d)] for a in range(5)]
            cross_low = [[before(up[a][b], d)] for a in range(5)]
            cross_up = [[after(low[a][b], d)] for a in range(5)]
            for a in range(5):
                value = -(dot_row(low[a], cross_low, 0) + dot_row(up[a], cross_up, 0))
                sys[25 + 5 * a + b] = value + 1.0 if a == b else value
                if level < 4:
                    sys[5 * a + b] = dot_row(low[a], low_column, 0)
                    sys[50 + 5 * a + b] = dot_row(up[a], up_column, 0)
    factors = factor([[sys[25 + 5 * a + b] for b in range(5)] for a in range(5)])

    arrived_r()
    values = unpack(recv_r, SOURCE, 10, lane)
    r = [values[a] + jnp.where(at_last, 0.0, after(values[5 + a], 1)) for a in range(5)]
    for level in range(5):
        d = 1 << level
        x = solve(kept_factors(fct2, level), r)
        x_low = [before(x[a], d) for a in range(5)]
        x_high = [after(x[a], d) for a in range(5)]
        r = []
        for a in range(5):
            low = [sol[level, 5 * a + b] for b in range(5)]
            up = [sol[level, 25 + 5 * a + b] for b in range(5)]
            r.append(x[a] + (dot_vec(low, x_low) + dot_vec(up, x_high)))
    ends = solve(factors, r)
    starts = [jnp.where(at_first, 0.0, before(x, 1)) for x in ends]
    pack(ends + starts, send_c, BACK, lane)
    start_c()
    arrived_c()
    values = unpack(recv_c, BACK, 10, lane)
    for f in range(5):
        xs[CX, f] = values[f]
        xs[0, f] = values[5 + f]

    g = apply_jacobian(cell(0), 1.0, [xs[0, f] for f in range(5)])
    x_right = [xs[CX, f] for f in range(5)]
    for m in reversed(range(7)):
        x_here = []
        for a in range(5):
            row_f = [fac[m, 5 * a + b] for b in range(5)]
            row_s = [fac[m, 25 + 5 * a + b] for b in range(5)]
            x_here.append((ys[m, a] + dot_vec(row_s, g)) + dot_vec(row_f, x_right))
            xs[2 * m + 2, a] = x_here[a]
        x_right = x_here

    def even(t, _):
        i = 2 * t + 1
        low_part = apply_jacobian(cell(i - 1), 1.0, [xs[i - 1, f] for f in range(5)])
        high_part = apply_jacobian(cell(i + 1), -1.0, [xs[i + 1, f] for f in range(5)])
        for f in range(5):
            xs[i, f] = 25.6 * (rr[i, f] + (low_part[f] - high_part[f]))
        return 0

    lax.fori_loop(0, 8, even, 0)

    def advance(i, _):
        new = [st[i, f] + xs[i, f] for f in range(5)]
        flux = apply_jacobian(cell(i), 0.0, new)
        for f in range(5):
            st[i, f] = new[f]
            lin[i, f] = flux[f]
        return 0

    for copy in halos:
        copy.wait_send()

    held = apply_jacobian(cell(CX - 1), 1.0, [xs[CX - 1, f] for f in range(5)])
    t = [rr[CX, f] + held[f] - (1.25 / 32.0) * xs[CX, f] for f in range(5)]
    u, v, w, k, h = cell(CX + 1)
    z = u - DISS
    z_inv = 1.0 / z
    p0 = t[1] - (z + u) * t[0]
    x2 = (t[2] - v * t[0]) * z_inv
    x3 = (t[3] - w * t[0]) * z_inv
    x4 = (t[4] - h * t[0] - u * p0) * z_inv
    x0 = (p0 - 0.4 * (x4 - u * t[0] - v * x2 - w * x3)) / (0.4 * (h - k) - z * z)
    beyond = [x0, t[0] + DISS * x0, x2 + v * x0, x3 + w * x0, x4 + (h - u * z) * x0]
    base = apply_jacobian(cell(CX + 1), 0.0, [st[CX + 1, f] for f in range(5)])
    for f in range(5):
        lin[CX + 1, f] = has_high * (base[f] + (t[f] + DISS * beyond[f]))
    lax.fori_loop(0, CX + 1, advance, 0)
    for f in range(5):
        lin[0, f] = has_low * lin[0, f]

    def differ(i, _):
        for f in range(5):
            xs[i, f] = -0.5 * (lin[i + 1, f] - lin[i - 1, f])
        return 0

    lax.fori_loop(1, CX + 1, differ, 0)
    for f in range(5):
        for half in range(2):
            place = pl.ds(8 * half, 8)
            next_ref[f, :, place, :] = jnp.swapaxes(st[pl.ds(1 + 8 * half, 8), f], 0, 1)
            diff_ref[f, :, place, :] = jnp.swapaxes(xs[pl.ds(1 + 8 * half, 8), f], 0, 1)

    sent_a()
    sent_b()
    sent_r()
    sent_c()


def on_device(state):
    def cells(*shape):
        return pltpu.VMEM(shape + (8, 128), F32)

    return pl.pallas_call(
        kernel,
        out_shape=(jax.ShapeDtypeStruct(state.shape, F32), jax.ShapeDtypeStruct(state.shape, F32)),
        in_specs=[pl.BlockSpec(memory_space=pltpu.VMEM)],
        out_specs=(pl.BlockSpec(memory_space=pltpu.VMEM), pl.BlockSpec(memory_space=pltpu.VMEM)),
        scratch_shapes=[
            cells(CX + 2, 5), cells(CX + 2, 5), cells(CX + 2, 5), cells(CX + 2, 5),
            cells(7, 50), cells(7, 5), cells(7, 30), cells(8, 25), cells(8, 50),
            cells(5), cells(5), cells(5),
            pltpu.VMEM((N * OWN[1], 128), F32), pltpu.VMEM((N * OWN[1], 128), F32),
            pltpu.VMEM((N * SHARE[1], 128), F32), pltpu.VMEM((N * SHARE[1], 128), F32),
            pltpu.VMEM((N * SOURCE[1], 128), F32), pltpu.VMEM((N * SOURCE[1], 128), F32),
            pltpu.VMEM((N * BACK[1], 128), F32), pltpu.VMEM((N * BACK[1], 128), F32),
            cells(75), cells(5, 50), cells(5, 30), cells(CX + 2, 5), cells(CX + 2, 5),
            pltpu.SemaphoreType.DMA((4,)), pltpu.SemaphoreType.DMA((4,)),
            pltpu.SemaphoreType.DMA((4,)), pltpu.SemaphoreType.DMA((4,)),
        ],
        compiler_params=pltpu.CompilerParams(
            collective_id=0, has_side_effects=True, vmem_limit_bytes=24 * 1024 * 1024
        ),
    )(state)


def solution(mesh):
    spec = P(None, None, "stream", "span")
    return jax.shard_map(
        on_device, mesh=mesh, in_specs=(spec,), out_specs=(spec, spec), check_vma=False
    )
```

```python
import jax
import jax.numpy as jnp
from jax import lax
from jax.experimental import pallas as pl
from jax.experimental.pallas import tpu as pltpu
from jax.sharding import PartitionSpec as P

MESH = pl.DeviceIdType.MESH
N = 32
SPAN = 8
CX = 16
DISS = 1.0 / 256.0
DIAG = 1.25 / 819.2
PIVOTS = (1, 2, 3, 0, 4)
OWN = (14, 16)
SHARE = (13, 16)
SOURCE = (3, 8)
BACK = (3, 8)
F32 = jnp.float32


STEPS = [(dx, dz) for dz in (4, 3, 5, 2, 6, 1, 7, 0) for dx in (2, 1, 3, 0) if dx or dz]


def mul(a, b):
    if a is None or b is None:
        return None
    if isinstance(a, float) and a == 1.0:
        return b
    if isinstance(b, float) and b == 1.0:
        return a
    return a * b


def add(a, b):
    if a is None:
        return b
    if b is None:
        return a
    return a + b


def sub(a, b):
    if b is None:
        return a
    if a is None:
        return -b
    return a - b


def primitives(s):
    inv = 1.0 / s[0]
    u, v, w = s[1] * inv, s[2] * inv, s[3] * inv
    k = 0.5 * (u * u + v * v + w * w)
    p = 0.4 * (s[4] - s[0] * k)
    return u, v, w, k, p, (s[4] + p) * inv


def apply_jacobian(cell, sign, x):
    u, v, w, k, h = cell
    us = u + sign * DISS if sign else u
    q = sub(x[1], mul(u, x[0]))
    inner = sub(mul(k, x[0]), mul(u, x[1]))
    inner = sub(sub(inner, mul(v, x[2])), mul(w, x[3]))
    p = mul(0.4, add(inner, x[4]))
    top = x[1]
    if sign and x[0] is not None:
        top = add(top, mul(sign * DISS, x[0]))
    return [
        top,
        add(add(mul(us, x[1]), mul(u, q)), p),
        add(mul(v, q), mul(us, x[2])),
        add(mul(w, q), mul(us, x[3])),
        add(add(mul(h, q), mul(us, x[4])), mul(u, p)),
    ]


def jacobian_columns(cell, sign):
    u, v, w, k, h = cell
    shift = sign * DISS
    us = u + shift
    gk = 0.4 * k
    gv, gw = -0.4 * v, -0.4 * w
    return [
        [shift, gk - u * u, -(u * v), -(u * w), u * (gk - h)],
        [1.0, 1.6 * u + shift, v, w, h - 0.4 * (u * u)],
        [None, gv, us, None, u * gv],
        [None, gw, None, us, u * gw],
        [None, 0.4, None, None, 1.4 * u + shift],
    ]


def product(left, left_sign, right, right_sign):
    columns = [apply_jacobian(left, left_sign, c) for c in jacobian_columns(right, right_sign)]
    return [[columns[j][i] for j in range(5)] for i in range(5)]


def full(x):
    if x is None:
        return jnp.zeros((8, 128), F32)
    if isinstance(x, float):
        return jnp.full((8, 128), x, F32)
    return x


def times_jacobian(t, cell):
    u, v, w, k, h = cell
    us = u + DISS
    alpha = (t[1] * u + t[2] * v) + (t[3] * w + t[4] * h)
    beta = 0.4 * (t[1] + u * t[4])
    return [
        (beta * k - u * alpha) + DISS * t[0],
        (t[0] + us * t[1]) + (alpha - beta * u),
        us * t[2] - beta * v,
        us * t[3] - beta * w,
        us * t[4] + beta,
    ]


def dot_row(row, matrix, j):
    total = row[0] * matrix[0][j]
    for i in range(1, 5):
        total = total + row[i] * matrix[i][j]
    return total


def dot_vec(row, x):
    total = row[0] * x[0]
    for i in range(1, 5):
        total = total + row[i] * x[i]
    return total


def factor(matrix):
    d = [[matrix[i][j] for j in PIVOTS] for i in PIVOTS]
    inverse = []
    low = [[None] * 5 for _ in range(5)]
    for k in range(5):
        inverse.append(1.0 / d[k][k])
        for i in range(k + 1, 5):
            low[i][k] = d[i][k] * inverse[k]
            for j in range(k + 1, 5):
                d[i][j] = d[i][j] - low[i][k] * d[k][j]
    return d, low, inverse


def keep_factors(factors, ref, m):
    d, low, inverse = factors
    kept = [d[k][j] for k in range(5) for j in range(k + 1, 5)]
    kept += [low[i][k] for k in range(5) for i in range(k + 1, 5)] + inverse
    for at, value in enumerate(kept):
        ref[m, at] = value


def kept_factors(ref, m):
    d, low = [[None] * 5 for _ in range(5)], [[None] * 5 for _ in range(5)]
    at = 0
    for k in range(5):
        for j in range(k + 1, 5):
            d[k][j] = ref[m, at]
            low[j][k] = ref[m, at + 10]
            at += 1
    return d, low, [ref[m, 20 + k] for k in range(5)]


def solve(factors, column):
    d, low, inverse = factors
    b = [column[i] for i in PIVOTS]
    for k in range(5):
        for i in range(k + 1, 5):
            b[i] = b[i] - low[i][k] * b[k]
    for k in reversed(range(5)):
        total = b[k]
        for j in range(k + 1, 5):
            total = total - d[k][j] * b[j]
        b[k] = total * inverse[k]
    x = [None] * 5
    for at, i in enumerate(PIVOTS):
        x[i] = b[at]
    return x


def quarters(c, lane):
    odd = (lane & 32) != 0
    high = (lane & 64) != 0

    def swap(a, b, mask, shift):
        return (
            jnp.where(mask, pltpu.roll(b, shift, 1), a),
            jnp.where(mask, b, pltpu.roll(a, 128 - shift, 1)),
        )

    c0, c1 = swap(c[0], c[1], odd, 32)
    c2, c3 = swap(c[2], c[3], odd, 32)
    c0, c2 = swap(c0, c2, high, 64)
    c1, c3 = swap(c1, c3, high, 64)
    return [c0, c1, c2, c3]


def pack(values, ref, rows, lane, places=(8, 1)):
    values = list(values)
    rows = rows[1]
    while len(values) % 4:
        values.append(values[-1])
    for g in range(len(values) // 4):
        out = quarters(values[4 * g : 4 * g + 4], lane)
        for t in range(4):
            ref[pl.ds(places[0] * t * rows + g, 8, stride=places[1] * rows), :] = out[t]


def unpack(ref, rows, count, lane, places=(8, 1)):
    values = []
    rows = rows[1]
    for g in range((count + 3) // 4):
        got = [
            ref[pl.ds(places[0] * t * rows + g, 8, stride=places[1] * rows), :] for t in range(4)
        ]
        values += quarters(got, lane)
    return values[:count]


def kernel(
    here, out_ref,
    st, pr, fx, rr, fac, ys, fct, lows, left, halo_send, halo_left, halo_right,
    send_a, recv_a, send_b, recv_b, send_r, recv_r, send_c, recv_c, sys, sol, fct2, xs, lin,
    ssem_h, rsem_h, ssem_x, rsem_x,
):
    me = lax.axis_index("stream")
    mine = lax.axis_index("span")
    span_right = (mine + 1) & (SPAN - 1)
    span_left = (mine + SPAN - 1) & (SPAN - 1)

    barrier = pltpu.get_barrier_semaphore()

    def stepped(dx, dz):
        return (((me >> 3) + dx) & 3) * 8 + ((me + dz) & 7)

    for step in STEPS:
        pl.semaphore_signal(
            barrier, inc=1, device_id=(stepped(*step), mine), device_id_type=MESH
        )
    for other in (span_left, span_right):
        pl.semaphore_signal(barrier, inc=1, device_id={"span": other}, device_id_type=MESH)

    lane = lax.broadcasted_iota(jnp.int32, (8, 128), 1)
    sub_row = lax.broadcasted_iota(jnp.int32, (8, 128), 0)

    for f in range(5):
        for half in range(2):
            st[pl.ds(1 + 8 * half, 8), f] = jnp.swapaxes(here[f, :, pl.ds(8 * half, 8), :], 0, 1)

    def prepare(i, _):
        s = [st[i, f] for f in range(5)]
        u, v, w, k, p, h = primitives(s)
        for at, value in enumerate((u, v, w, k, h)):
            pr[i, at] = value
        flux = [s[1], s[1] * u + p, s[2] * u, s[3] * u, u * (s[4] + p)]
        for f in range(5):
            fx[i, f] = flux[f]
        return 0

    lax.fori_loop(1, CX + 1, prepare, 0)

    def cell(i):
        return tuple(pr[i, at] for at in range(5))

    def eliminate(m, first_node):
        i = 2 * m + 2
        below1, middle, above1, above2 = (cell(i + t) for t in range(-1, 3))
        upper = [[full(x) for x in row] for row in product(above1, -1.0, above2, -1.0)]
        first = product(below1, 1.0, middle, -1.0)
        second = product(above1, -1.0, middle, 1.0)
        diag = [[full(add(first[a][b], second[a][b])) for b in range(5)] for a in range(5)]
        if first_node:
            columns = jacobian_columns(below1, 1.0)
            spike = [[full(columns[b][a]) for b in range(5)] for a in range(5)]
        else:
            low = [[full(x) for x in row] for row in product(below1, 1.0, cell(i - 2), 1.0)]
            f_before = [[fac[m - 1, 5 * a + b] for b in range(5)] for a in range(5)]
            for a in range(5):
                for b in range(5):
                    lows[m, 5 * a + b] = low[a][b]
                    diag[a][b] = diag[a][b] - dot_row(low[a], f_before, b)
        for a in range(5):
            diag[a][a] = diag[a][a] + DIAG
        factors = factor(diag)
        keep_factors(factors, fct, m)
        for b in range(5):
            x = solve(factors, [upper[a][b] for a in range(5)])
            for a in range(5):
                fac[m, 5 * a + b] = x[a]
        if not first_node:
            s_before = [[fac[m - 1, 25 + 5 * a + b] for b in range(5)] for a in range(5)]
            spike = [[dot_row(low[a], s_before, b) for b in range(5)] for a in range(5)]
        for b in range(5):
            x = solve(factors, [spike[a][b] for a in range(5)])
            for a in range(5):
                fac[m, 25 + 5 * a + b] = x[a]

    def eliminate_step(m, _):
        eliminate(m, False)
        return 0

    eliminate(0, True)
    lax.fori_loop(1, 7, eliminate_step, 0)

    low = [[full(x) for x in row] for row in product(cell(CX - 1), 1.0, cell(CX - 2), 1.0)]
    own = product(cell(CX - 1), 1.0, cell(CX), -1.0)
    f_last = [[fac[6, 5 * a + b] for b in range(5)] for a in range(5)]
    s_last = [[fac[6, 25 + 5 * a + b] for b in range(5)] for a in range(5)]
    to_low = [dot_row(low[a], s_last, b) for a in range(5) for b in range(5)]
    to_own = []
    for a in range(5):
        for b in range(5):
            lows[7, 5 * a + b] = low[a][b]
            value = full(own[a][b]) - dot_row(low[a], f_last, b)
            to_own.append(value + DIAG if a == b else value)
    pack(to_low + to_own + list(cell(CX)), send_a, OWN, lane)

    for f in range(5):
        packed = st[1, f]
        for i in range(CX):
            moved = pltpu.roll(st[1 + i, f], (2 + 4 * i) % 128, 1)
            packed = jnp.where((lane >> 2) == i, moved, packed)
        halo_send[f] = packed

    pl.semaphore_wait(barrier, N - 1 + 2)

    halos = []
    for at, (src, dst, who) in enumerate(
        (
            (st.at[CX], st.at[0], {"stream": (me + 1) & (N - 1)}),
            (st.at[1], st.at[CX + 1], {"stream": (me + N - 1) & (N - 1)}),
            (halo_send, halo_left, {"span": span_right}),
            (halo_send, halo_right, {"span": span_left}),
        )
    ):
        copy = pltpu.make_async_remote_copy(
            src_ref=src, dst_ref=dst, send_sem=ssem_h.at[at], recv_sem=rsem_h.at[at],
            device_id=who, device_id_type=MESH,
        )
        copy.start()
        halos.append(copy)

    def exchange(send, recv, at, rows):
        count, stride = rows

        def start():
            def send_to(other):
                pltpu.make_async_remote_copy(
                    src_ref=send.at[pl.ds(pl.multiple_of(other * stride, 8), count)],
                    dst_ref=recv.at[pl.ds(pl.multiple_of(me * stride, 8), count)],
                    send_sem=ssem_x.at[at], recv_sem=rsem_x.at[at],
                    device_id=(other, mine), device_id_type=MESH,
                ).start()

            for step in STEPS:
                send_to(stepped(*step))
            place = pl.ds(pl.multiple_of(me * stride, 8), stride)
            recv[place, :] = send[place, :]

        everything = pltpu.make_async_remote_copy(
            src_ref=send.at[pl.ds(0, (N - 1) * count)],
            dst_ref=recv.at[pl.ds(0, (N - 1) * count)],
            send_sem=ssem_x.at[at], recv_sem=rsem_x.at[at],
            device_id=((me + 1) & (N - 1), mine), device_id_type=MESH,
        )
        return start, everything.wait_recv, everything.wait_send

    start_a, arrived_a, sent_a = exchange(send_a, recv_a, 0, OWN)
    start_b, arrived_b, sent_b = exchange(send_b, recv_b, 1, SHARE)
    start_r, arrived_r, sent_r = exchange(send_r, recv_r, 2, SOURCE)
    start_c, arrived_c, sent_c = exchange(send_c, recv_c, 3, BACK)
    start_a()

    upper = product(cell(1), -1.0, cell(2), -1.0)
    columns = jacobian_columns(cell(1), -1.0)
    for a in range(5):
        for b in range(5):
            left[0, 5 * a + b] = full(upper[a][b])
            left[0, 25 + 5 * a + b] = full(columns[b][a])

    def follow(m, _):
        f_here = [[fac[m, 5 * a + b] for b in range(5)] for a in range(5)]
        s_here = [[fac[m, 25 + 5 * a + b] for b in range(5)] for a in range(5)]
        for a in range(5):
            row = [left[m, 5 * a + b] for b in range(5)]
            for b in range(5):
                left[m + 1, 25 + 5 * a + b] = left[m, 25 + 5 * a + b] - dot_row(row, s_here, b)
                left[m + 1, 5 * a + b] = dot_row(row, f_here, b)
        return 0

    lax.fori_loop(0, 7, follow, 0)
    pack([left[7, at] for at in range(50)], send_b, SHARE, lane)
    start_b()

    for copy in halos:
        copy.wait_recv()
    prepare(0, 0)
    prepare(CX + 1, 0)

    has_low = jnp.where(me > 0, 1.0, 0.0).astype(F32)
    has_high = jnp.where(me < N - 1, 1.0, 0.0).astype(F32)

    rim = [jnp.where((lane & 2) == 0, halo_left[f], halo_right[f]) for f in range(5)]
    _, v, _, _, p, _ = primitives(rim)
    rim_flux = [rim[2], rim[1] * v, rim[2] * v + p, rim[3] * v, v * (rim[4] + p)]
    for f in range(5):
        for i in range(CX):
            xs[1 + i, f] = pltpu.roll(rim_flux[f], (254 - 4 * i) % 128, 1)

    def right_side(i, _):
        s = [st[i, f] for f in range(5)]
        u, v, w, k, h = (pr[i, at] for at in range(5))
        total = h * s[0]
        p = total - s[4]
        g = [s[2], s[1] * v, s[2] * v + p, s[3] * v, v * total]
        wall = [s[3], s[1] * w, s[2] * w, s[3] * w + p, w * total]
        low = jnp.where(i == 1, has_low, 1.0)
        high = jnp.where(i == CX, has_high, 1.0)
        for f in range(5):
            edge = xs[i, f]
            near = pltpu.roll(jnp.where(lane < 1, edge, g[f]), 127, 1) - pltpu.roll(
                jnp.where(lane >= 127, edge, g[f]), 1, 1
            )
            far = pltpu.roll(jnp.where(lane < 2, edge, g[f]), 126, 1) - pltpu.roll(
                jnp.where(lane >= 126, edge, g[f]), 2, 1
            )
            span = 8.0 * near - far
            mirrored = wall[f] if f == 3 else -wall[f]
            above = jnp.where(sub_row == 7, wall[f], pltpu.roll(wall[f], 7, 0))
            below = jnp.where(sub_row == 0, mirrored, pltpu.roll(wall[f], 1, 0))
            stream = fx[i + 1, f] * high - fx[i - 1, f] * low
            curve = st[i + 1, f] * high + st[i - 1, f] * low - 2.0 * s[f]
            rr[i, f] = (
                DISS * curve - stream - (1.0 / 384.0) * span - (1.0 / 64.0) * (above - below)
            )
        return 0

    lax.fori_loop(1, CX + 1, right_side, 0)

    def source(i):
        return [rr[i, f] for f in range(5)]

    y = None
    r_first = apply_jacobian(cell(1), -1.0, source(1))
    to_left = [-r_first[a] for a in range(5)]
    for m in range(8):
        i = 2 * m + 2
        r_here = source(i)
        r_low = apply_jacobian(cell(i - 1), 1.0, source(i - 1))
        column = [(1.0 / 25.6) * r_here[a] + r_low[a] for a in range(5)]
        if m < 7:
            r_high = apply_jacobian(cell(i + 1), -1.0, source(i + 1))
            column = [column[a] - r_high[a] for a in range(5)]
        if m > 0:
            column = [
                column[a] + dot_vec([lows[m, 5 * a + b] for b in range(5)], y) for a in range(5)
            ]
        if m < 7:
            y = solve(kept_factors(fct, m), column)
            for a in range(5):
                ys[m, a] = y[a]
                row = [left[m, 5 * a + b] for b in range(5)]
                to_left[a] = to_left[a] + dot_vec(row, y)
    pack(column + to_left, send_r, SOURCE, lane)
    start_r()

    at_first = (sub_row == 0) & (lane < 32)
    at_last = (sub_row == 7) & (lane >= 96)

    def after(x, d):
        if d >= 4:
            return pltpu.roll(x, 8 - d // 4, 0)
        x = pltpu.roll(x, 128 - 32 * d, 1)
        return jnp.where(lane >= 128 - 32 * d, pltpu.roll(x, 7, 0), x)

    def before(x, d):
        if d >= 4:
            return pltpu.roll(x, d // 4, 0)
        x = pltpu.roll(x, 32 * d, 1)
        return jnp.where(lane < 32 * d, pltpu.roll(x, 1, 0), x)

    arrived_a()
    values = unpack(recv_a, OWN, 55, lane, (1, 4))
    last_cell = values[50:]
    cell_before = [before(x, 1) for x in last_cell]
    for a in range(5):
        low = times_jacobian(values[5 * a : 5 * a + 5], cell_before)
        for b in range(5):
            sys[5 * a + b] = jnp.where(at_first, 0.0, low[b])
            sys[25 + 5 * a + b] = values[25 + 5 * a + b]
    arrived_b()
    values = unpack(recv_b, SHARE, 50, lane, (1, 4))
    for a in range(5):
        share = [jnp.where(at_last, 0.0, after(values[25 + 5 * a + b], 1)) for b in range(5)]
        share = times_jacobian(share, last_cell)
        for b in range(5):
            sys[25 + 5 * a + b] = sys[25 + 5 * a + b] + share[b]
            sys[50 + 5 * a + b] = jnp.where(at_last, 0.0, after(values[5 * a + b], 1))

    for level in range(5):
        d = 1 << level
        factors = factor([[sys[25 + 5 * a + b] for b in range(5)] for a in range(5)])
        keep_factors(factors, fct2, level)
        for b in range(5):
            x = solve(factors, [sys[5 * a + b] for a in range(5)])
            for a in range(5):
                sol[level, 5 * a + b] = x[a]
            x = solve(factors, [sys[50 + 5 * a + b] for a in range(5)])
            for a in range(5):
                sol[level, 25 + 5 * a + b] = x[a]
        low = [[sol[level, 5 * a + b] for b in range(5)] for a in range(5)]
        up = [[sol[level, 25 + 5 * a + b] for b in range(5)] for a in range(5)]
        for b in range(5):
            low_column = [[before(low[a][b], d)] for a in range(5)]
            up_column = [[after(up[a][b], d)] for a in range(5)]
            cross_low = [[before(up[a][b], d)] for a in range(5)]
            cross_up = [[after(low[a][b], d)] for a in range(5)]
            for a in range(5):
                value = -(dot_row(low[a], cross_low, 0) + dot_row(up[a], cross_up, 0))
                sys[25 + 5 * a + b] = value + 1.0 if a == b else value
                if level < 4:
                    sys[5 * a + b] = dot_row(low[a], low_column, 0)
                    sys[50 + 5 * a + b] = dot_row(up[a], up_column, 0)
    factors = factor([[sys[25 + 5 * a + b] for b in range(5)] for a in range(5)])

    arrived_r()
    values = unpack(recv_r, SOURCE, 10, lane, (1, 4))
    r = [values[a] + jnp.where(at_last, 0.0, after(values[5 + a], 1)) for a in range(5)]
    for level in range(5):
        d = 1 << level
        x = solve(kept_factors(fct2, level), r)
        x_low = [before(x[a], d) for a in range(5)]
        x_high = [after(x[a], d) for a in range(5)]
        r = []
        for a in range(5):
            low = [sol[level, 5 * a + b] for b in range(5)]
            up = [sol[level, 25 + 5 * a + b] for b in range(5)]
            r.append(x[a] + (dot_vec(low, x_low) + dot_vec(up, x_high)))
    ends = solve(factors, r)
    starts = [jnp.where(at_first, 0.0, before(x, 1)) for x in ends]
    pack(ends + starts, send_c, BACK, lane, (1, 4))
    start_c()
    arrived_c()
    values = unpack(recv_c, BACK, 10, lane)
    for f in range(5):
        xs[CX, f] = values[f]
        xs[0, f] = values[5 + f]

    g = apply_jacobian(cell(0), 1.0, [xs[0, f] for f in range(5)])
    x_right = [xs[CX, f] for f in range(5)]
    for m in reversed(range(7)):
        x_here = []
        for a in range(5):
            row_f = [fac[m, 5 * a + b] for b in range(5)]
            row_s = [fac[m, 25 + 5 * a + b] for b in range(5)]
            x_here.append((ys[m, a] + dot_vec(row_s, g)) + dot_vec(row_f, x_right))
            xs[2 * m + 2, a] = x_here[a]
        x_right = x_here

    def even(t, _):
        i = 2 * t + 1
        low_part = apply_jacobian(cell(i - 1), 1.0, [xs[i - 1, f] for f in range(5)])
        high_part = apply_jacobian(cell(i + 1), -1.0, [xs[i + 1, f] for f in range(5)])
        for f in range(5):
            xs[i, f] = 25.6 * (rr[i, f] + (low_part[f] - high_part[f]))
        return 0

    lax.fori_loop(0, 8, even, 0)

    def advance(i, _):
        new = [st[i, f] + xs[i, f] for f in range(5)]
        flux = apply_jacobian(cell(i), 0.0, new)
        for f in range(5):
            st[i, f] = new[f]
            lin[i, f] = flux[f]
        return 0

    for copy in halos:
        copy.wait_send()

    held = apply_jacobian(cell(CX - 1), 1.0, [xs[CX - 1, f] for f in range(5)])
    t = [rr[CX, f] + held[f] - (1.25 / 32.0) * xs[CX, f] for f in range(5)]
    u, v, w, k, h = cell(CX + 1)
    z = u - DISS
    z_inv = 1.0 / z
    p0 = t[1] - (z + u) * t[0]
    x2 = (t[2] - v * t[0]) * z_inv
    x3 = (t[3] - w * t[0]) * z_inv
    x4 = (t[4] - h * t[0] - u * p0) * z_inv
    x0 = (p0 - 0.4 * (x4 - u * t[0] - v * x2 - w * x3)) / (0.4 * (h - k) - z * z)
    beyond = [x0, t[0] + DISS * x0, x2 + v * x0, x3 + w * x0, x4 + (h - u * z) * x0]
    base = apply_jacobian(cell(CX + 1), 0.0, [st[CX + 1, f] for f in range(5)])
    for f in range(5):
        lin[CX + 1, f] = has_high * (base[f] + (t[f] + DISS * beyond[f]))
    lax.fori_loop(0, CX + 1, advance, 0)
    for f in range(5):
        lin[0, f] = has_low * lin[0, f]

    def differ(i, _):
        for f in range(5):
            xs[i, f] = -0.5 * (lin[i + 1, f] - lin[i - 1, f])
        return 0

    lax.fori_loop(1, CX + 1, differ, 0)
    for f in range(5):
        for half in range(2):
            place = pl.ds(8 * half, 8)
            out_ref[0, f, :, place, :] = jnp.swapaxes(st[pl.ds(1 + 8 * half, 8), f], 0, 1)
            out_ref[1, f, :, place, :] = jnp.swapaxes(xs[pl.ds(1 + 8 * half, 8), f], 0, 1)

    sent_a()
    sent_b()
    sent_r()
    sent_c()


def on_device(state):
    def cells(*shape):
        return pltpu.VMEM(shape + (8, 128), F32)

    both = pl.pallas_call(
        kernel,
        out_shape=jax.ShapeDtypeStruct((2,) + state.shape, F32),
        in_specs=[pl.BlockSpec(memory_space=pltpu.VMEM)],
        out_specs=pl.BlockSpec(memory_space=pltpu.VMEM),
        scratch_shapes=[
            cells(CX + 2, 5), cells(CX + 2, 5), cells(CX + 2, 5), cells(CX + 2, 5),
            cells(7, 50), cells(7, 5), cells(7, 30), cells(8, 25), cells(8, 50),
            cells(5), cells(5), cells(5),
            pltpu.VMEM((N * OWN[1], 128), F32), pltpu.VMEM((N * OWN[1], 128), F32),
            pltpu.VMEM((N * SHARE[1], 128), F32), pltpu.VMEM((N * SHARE[1], 128), F32),
            pltpu.VMEM((N * SOURCE[1], 128), F32), pltpu.VMEM((N * SOURCE[1], 128), F32),
            pltpu.VMEM((N * BACK[1], 128), F32), pltpu.VMEM((N * BACK[1], 128), F32),
            cells(75), cells(5, 50), cells(5, 30), cells(CX + 2, 5), cells(CX + 2, 5),
            pltpu.SemaphoreType.DMA((4,)), pltpu.SemaphoreType.DMA((4,)),
            pltpu.SemaphoreType.DMA((4,)), pltpu.SemaphoreType.DMA((4,)),
        ],
        compiler_params=pltpu.CompilerParams(
            collective_id=0, has_side_effects=True, vmem_limit_bytes=24 * 1024 * 1024
        ),
    )(state)
    return both[0], both[1]


def solution(mesh):
    spec = P(None, None, "stream", "span")
    return jax.shard_map(
        on_device, mesh=mesh, in_specs=(spec,), out_specs=(spec, spec), check_vma=False
    )
```
